256 devices in a mesh: pole: 8 (over z_hi, core), row: 8 (over y, z_lo), col: 4 (over x).
Axes of the slice: x: 4, y: 4, z: 8 (z_hi: 4, z_lo: 2; z = z_hi * 2 + z_lo), core: 2. Of those that a mesh axis runs over, the one named last changes fastest.
Arguments:
- ancestor_inverse: bfloat16 [8, 6144, 6144], P('pole', 'row', 'col'), may hold values from -0.078125 to 0.078125
- factor_cols: bfloat16 [8, 6144, 4096], P('pole', None, ('row', 'col')), may hold values from -6 to 6
- diag_inverse: float32 [8, 4096], P('pole', ('row', 'col')), may hold values from 20 to 200
- pole_weights: float32 [8], P('pole'), may hold values from 0.004 to 0.02
- block_pattern: int32 [48, 32], replicated, may hold values 0 or 1
- supernode_ids: int32 [4096], replicated, may hold values from 0 to 31, never falling along the last dimension, each value on 1 to 2048 neighbouring positions
Outputs:
- inverse_block: bfloat16 [8, 6144, 8, 4, 128], P('pole', 'row', None, 'col')
- density_diag: float32 [4096], P(('row', 'col'))
The draws below stay inside these ranges and needn't reach their ends.
Inputs may be any that keep to these rules, and one draw needn't show every extreme that they name: `supernode_ids`: never falling along the columns; each supernode has 1 to 2048 columns, one exactly 2048.
All inputs are finite; a program needn't handle non-finite values.
Results may differ from the reference program's by a relative error of at most 0.001.
Values may be sent and summed in bfloat16 or wider, within the bound.
A program may use at most 192 MiB of HBM per device.

```python
import math
import jax
import jax.numpy as jnp
import numpy as np
from jax import lax

NC = 6144
KB = 128
RBLK = 128
NSUP = 32
POLES = 8
K = 4096
NRB = 48
MOST = 2048
N_ROW = 8
N_COL = 4


def plant(result, stream_key, least, largest):
    index_at = [jax.random.randint(jax.random.fold_in(stream_key, axis), (), 0, length) for axis, length in enumerate(result.shape)]
    longest = result.shape.index(max(result.shape))
    neighbour = index_at[:longest] + [(index_at[longest] + 1) % result.shape[longest]] + index_at[longest + 1:]
    return result.at[tuple(index_at)].set(least).at[tuple(neighbour)].set(largest)


def shard_levels(own_key, extent, split, least, high):
    def one(dim, parts):
        heights = jax.random.uniform(jax.random.fold_in(jax.random.fold_in(own_key, 6), dim), (parts,), jnp.float32, least / len(split), high / len(split))
        return jnp.repeat(jnp.exp(heights), extent[dim] // parts).reshape((-1,) + (1,) * (len(extent) - dim - 1))

    level = one(*split[0])
    for cut in split[1:]:
        level = level * one(*cut)
    return level


def profile(number_of, total, most, slope):
    portions = [(1 << 20) // math.isqrt(rank ** slope) + 1 for rank in range(2, number_of + 1)]
    rest, given = total - most - (number_of - 1), [1] * (number_of - 1)
    while rest > 0:
        movable = [i for i in range(number_of - 1) if given[i] < most]
        whole, left = sum([portions[i] for i in movable]), rest
        for i in movable:
            extra = min(most - given[i], max(1, left * portions[i] // whole), rest)
            given[i] = given[i] + extra
            rest = rest - extra
    return np.array([most] + given)


def ragged_sizes(key, count, total, reach, skew):
    if count == 2:
        one = jax.random.randint(key, (), max(1, total - reach), min(reach, total - 1) + 1)
        return jnp.stack([one, total - one])
    lengths = jnp.asarray(profile(count, total, reach, skew), jnp.int32)
    pairs = (count - 1) // 2
    donor, receiver = lengths[1:1 + 2 * pairs:2], lengths[2:2 + 2 * pairs:2]
    margin = jnp.minimum(donor - 1, reach - receiver)
    moved = jax.random.randint(jax.random.fold_in(key, 1), (pairs,), 0, 1 << 20) % (margin + 1)
    lengths = lengths.at[1:1 + 2 * pairs:2].set(donor - moved).at[2:2 + 2 * pairs:2].set(receiver + moved)
    return lengths[jax.random.permutation(jax.random.fold_in(key, 2), count)]


def scatter_about(rng, shape, scale, most, pieces=(), kind=jnp.bfloat16):
    values = jax.random.normal(rng, shape, jnp.float32) * scale
    if len(pieces) > 0:
        values = shard_levels(rng, shape, pieces, -0.22, 0.18) * values
    return jnp.clip(values, min=-most, max=most).astype(kind)


def setup_inputs(seed: int = 0) -> dict:
    key_list = jax.random.split(jax.random.key(seed), 7)
    return {
        "ancestor_inverse": scatter_about(key_list[0], (POLES, NC, NC), NC ** -0.5, 0.078125, ((0, 8), (1, 8), (2, 4))),
        "factor_cols": scatter_about(key_list[1], (POLES, NC, K), 1.0, 6.0, ((0, 8), (2, 32))),
        "diag_inverse": jnp.clip(jnp.exp(math.log(200.0) - 2.3025851 * jax.random.uniform(key_list[2], (POLES, K), jnp.float32) ** shard_levels(key_list[2], (POLES, K), ((0, 8), (1, 32)), -0.2, 0.2)), 20.0, 200.0),
        "pole_weights": jnp.clip(0.004 + 0.015999999 * jax.random.uniform(key_list[3], (POLES,), jnp.float32) ** shard_levels(key_list[3], (POLES,), ((0, 8),), -0.2, 0.2), 0.004, 0.02),
        "block_pattern": plant((jax.random.randint(key_list[4], (NRB, NSUP), 0, 2) < 1).astype(jnp.int32), jax.random.fold_in(key_list[4], 1), 0, 1),
        "supernode_ids": jnp.searchsorted(jnp.cumsum(ragged_sizes(key_list[5], NSUP, K, MOST, 2)), jnp.arange(K), side="right").astype(jnp.int32),
    }


def pattern_mask(block_pattern, supernode_ids):
    onehot = (supernode_ids[None, :] == jnp.arange(NSUP, dtype=jnp.int32)[:, None]).astype(jnp.float32)
    coarse = jnp.dot(block_pattern.astype(jnp.float32), onehot, precision=lax.Precision.HIGHEST)
    return jnp.repeat(coarse, RBLK, axis=0).astype(jnp.bfloat16)


def reference(ancestor_inverse, factor_cols, diag_inverse, pole_weights, block_pattern, supernode_ids):
    entry_mask = pattern_mask(block_pattern, supernode_ids)

    def one_pole(pole_index):
        masked = factor_cols[pole_index] * entry_mask
        product = jnp.dot(ancestor_inverse[pole_index].astype(jnp.float32), masked.astype(jnp.float32), precision=lax.Precision.HIGHEST)
        inner_sums = jnp.sum(masked.astype(jnp.float32) * product, axis=0)
        weighted = pole_weights[pole_index] * (diag_inverse[pole_index] + inner_sums)
        return (-product).astype(jnp.bfloat16), weighted

    outputs, weighted = lax.map(one_pole, jnp.arange(POLES, dtype=jnp.int32))
    inverse_block = outputs.reshape(POLES, NC, N_ROW, N_COL, KB)
    return inverse_block, jnp.sum(weighted, axis=0)
```

```python
import functools

import jax
import jax.numpy as jnp
from jax import lax
from jax.experimental import pallas as pl
from jax.experimental.pallas import tpu as pltpu
from jax.sharding import PartitionSpec as P

MESH = pl.DeviceIdType.MESH
F32, BF16 = jnp.float32, jnp.bfloat16

UNITS = 24
SLOTS = [(dy, dz) for dy in range(4) for dz in range(2)]
OWN, ZP, YN, YP, YF = (0, 0), (0, 1), (1, 0), (3, 0), (2, 0)
YNZ, YPZ, YFZ = (1, 1), (3, 1), (2, 1)
PAIRS = [(OWN, ZP), (YN, YP), (YNZ, YPZ), (YF, YFZ)]

QUARTER = [(0, 6), (6, 6), (12, 6), (18, 6)]
Y_UP = (
    [(OWN, YP, s, n) for s, n in QUARTER]
    + [(YP, YF, 0, 6), (YP, YF, 6, 6)]
    + [(ZP, YPZ, 0, 6), (ZP, YPZ, 6, 6), (ZP, YPZ, 12, 2)]
    + [(YPZ, YFZ, 0, 4), (YPZ, YFZ, 4, 2)]
)
Y_DOWN = (
    [(OWN, YN, s, n) for s, n in QUARTER[2:] + QUARTER[:2]]
    + [(YN, YF, 12, 6), (YN, YF, 18, 6)]
    + [(ZP, YNZ, 6, 6), (ZP, YNZ, 0, 6), (ZP, YNZ, 12, 2)]
    + [(YNZ, YFZ, 6, 4), (YNZ, YFZ, 10, 2)]
)
Z_SWAP = (
    [(OWN, ZP, s, n) for s, n in QUARTER]
    + [(YN, YNZ, 14, 10), (YP, YPZ, 14, 10)]
    + [(YF, YFZ, 12, 6), (YF, YFZ, 18, 4), (YF, YFZ, 22, 2)]
)
X_UP = [(0, 3, m) for m in (0, 1, 2, 3, 4, 5)] + [(3, 2, m) for m in (0, 1, 2)]
X_DOWN = [(0, 1, m) for m in (3, 4, 5, 0, 1, 2)] + [(1, 2, m) for m in (3, 4, 5)]


def at_slot(slot):
    return slot[0] * 2 + slot[1]


def kernel(
    a_hbm, f_hbm, diag_ref, weight_ref, pattern_ref, ids_ref,
    out_hbm, density_ref,
    a_all, f_all, acc, coarse, out_vmem, part, red, pol,
    load_sem, out_sem, f_send, f_recv, a_send, a_recv, red_send, red_recv, pol_send, pol_recv,
):
    pole, row, col = lax.axis_index("pole"), lax.axis_index("row"), lax.axis_index("col")
    n_pole = lax.axis_size("pole")
    y, z = row // 2, row % 2
    rows, depth = a_all.shape[1], a_all.shape[2]
    unit, sixth = f_all.shape[1] // UNITS, rows // 6
    blocks = coarse.shape[0] // 4
    rblk = depth // blocks

    def row_of(slot):
        return ((y + slot[0]) % 4) * 2 + (z + slot[1]) % 2

    x_up, x_down = {"col": (col + 1) % 4}, {"col": (col + 3) % 4}
    y_up, y_down, z_swap = {"row": row_of(YN)}, {"row": row_of(YP)}, {"row": row_of(ZP)}

    own_rows = pltpu.make_async_copy(a_hbm.at[0], a_all.at[0], load_sem.at[4])
    loads = []
    for q in range(4):
        source = pl.ds(pl.multiple_of(((col + q) % 4) * depth, depth), depth)
        loads.append(
            pltpu.make_async_copy(f_hbm.at[0, source], f_all.at[0, pl.ds(q * depth, depth)], load_sem.at[q])
        )
    for load in loads:
        load.start()
    own_rows.start()

    barrier = pltpu.get_barrier_semaphore()
    friends = [x_up, x_down]
    friends += [{"row": row_of(slot)} for slot in SLOTS[1:]]
    friends += [{"pole": (pole + d) % n_pole} for d in range(1, n_pole)]
    for friend in friends:
        pl.semaphore_signal(barrier, inc=1, device_id=friend, device_id_type=MESH)
    pl.semaphore_wait(barrier, len(friends))

    def f_copies(link, plan, device):
        copies = []
        for i, (here, there, first, count) in enumerate(plan):
            span = pl.ds(first * unit, count * unit)
            copies.append(
                pltpu.make_async_remote_copy(
                    src_ref=f_all.at[at_slot(here), span],
                    dst_ref=f_all.at[at_slot(there), span],
                    send_sem=f_send.at[link, i],
                    recv_sem=f_recv.at[link, i],
                    device_id=device,
                    device_id_type=MESH,
                )
            )
        return copies

    def a_copies(link, plan, device):
        copies = []
        for i, (here, there, m) in enumerate(plan):
            span = pl.ds(m * sixth, sixth)
            copies.append(
                pltpu.make_async_remote_copy(
                    src_ref=a_hbm.at[0, span] if here == 0 else a_all.at[here, span],
                    dst_ref=a_all.at[there, span],
                    send_sem=a_send.at[link, i],
                    recv_sem=a_recv.at[link, i],
                    device_id=device,
                    device_id_type=MESH,
                )
            )
        return copies

    yu, yd, zs = f_copies(0, Y_UP, y_up), f_copies(1, Y_DOWN, y_down), f_copies(2, Z_SWAP, z_swap)
    xu, xd = a_copies(0, X_UP, x_up), a_copies(1, X_DOWN, x_down)

    def start(copies, *which):
        for i in which:
            copies[i].start()

    def arrived(copies, *which):
        for i in which:
            copies[i].wait_recv()

    start(xu, 0)
    start(xd, 0)

    ids = ids_ref[pl.ds(row * 4 + col, 1), :]
    onehot = jnp.where(ids == lax.broadcasted_iota(jnp.int32, (pattern_ref.shape[0], ids.shape[1]), 0), 1.0, 0.0)
    coarse[...] = lax.dot_general(
        pattern_ref[...].astype(F32).astype(BF16), onehot.astype(BF16), (((0,), (0,)), ((), ())),
        preferred_element_type=F32,
    )

    def mask_quarter(q):
        loads[q].wait()
        first = ((col + q) % 4) * blocks

        def body(j, carry):
            span = pl.ds(pl.multiple_of(q * depth + j * rblk, rblk), rblk)
            mask = coarse[pl.ds(first + j, 1), :].astype(BF16)
            f_all[0, span, :] = f_all[0, span, :] * mask
            return carry

        lax.fori_loop(0, blocks, body, 0)

    mask_quarter(0)
    start(yu, 0)
    start(zs, 0)
    mask_quarter(2)
    start(yd, 0)
    mask_quarter(1)
    start(yu, 1)
    start(zs, 1)
    start(xu, 1)
    start(xd, 1)
    mask_quarter(3)
    start(yd, 1)
    start(yu, 2)
    start(zs, 2)
    start(yd, 2)
    start(xu, 2)
    start(xd, 2)
    start(yu, 3)
    start(zs, 3)
    start(yd, 3)
    start(xu, 3, 4, 5)
    start(xd, 3, 4, 5)

    def multiply(pair, q):
        span = slice(q * depth, (q + 1) * depth)
        right = jnp.concatenate([f_all[at_slot(s), span, :] for s in PAIRS[pair]], axis=1)
        product = jnp.dot(a_all[q], right, preferred_element_type=F32)
        if q == 0:
            acc[pair] = product
        else:
            acc[pair] = acc[pair] + product

    own_span = pl.ds(pl.multiple_of(((row * rows // depth - col + 4) % 4) * depth + (row * rows) % depth, rows), rows)
    outs, reds = [], []

    def finish(pair):
        for half, slot in enumerate(PAIRS[pair]):
            s = at_slot(slot)
            product = acc[pair, :, half * 128 : (half + 1) * 128]
            out_vmem[s] = (-product).astype(BF16)
            columns = pl.ds(pl.multiple_of(row_of(slot) * 128, 128), 128)
            outs.append(pltpu.make_async_copy(out_vmem.at[s], out_hbm.at[:, columns], out_sem.at[s]))
            outs[-1].start()
            terms = f_all[s, own_span, :].astype(F32) * product
            sums = jnp.sum(terms.reshape(rows // 8, 8, 128), axis=0)
            if slot == OWN:
                red[0] = sums
                continue
            part[s] = sums
            back = at_slot(((-slot[0]) % 4, slot[1]))
            copy = pltpu.make_async_remote_copy(
                src_ref=part.at[s],
                dst_ref=red.at[back],
                send_sem=red_send.at[s],
                recv_sem=red_recv.at[back],
                device_id={"row": row_of(slot)},
                device_id_type=MESH,
            )
            copy.start()
            reds.append(copy)

    own_rows.wait()
    arrived(zs, 0)
    multiply(0, 0)
    arrived(yu, 0, 1)
    start(yu, 4, 5)
    arrived(yd, 0, 1)
    start(yd, 4, 5)
    arrived(xu, 0, 1, 2)
    start(xu, 6, 7, 8)
    arrived(xd, 0, 1, 2)
    start(xd, 6, 7, 8)
    arrived(zs, 1, 2, 3)
    start(yu, 6, 7, 8)
    start(yd, 6, 7, 8)
    arrived(yu, 2, 3)
    arrived(yd, 2, 3)
    start(zs, 4, 5)
    multiply(1, 0)
    arrived(yu, 4, 5)
    arrived(yd, 4, 5)
    start(zs, 6, 7, 8)
    arrived(xu, 3, 4, 5)
    arrived(xd, 3, 4, 5)
    multiply(0, 1)
    multiply(0, 3)
    arrived(yu, 6)
    start(yu, 9, 10)
    arrived(yd, 6)
    start(yd, 9, 10)
    multiply(1, 1)
    multiply(1, 3)
    arrived(zs, 4, 5)
    arrived(yu, 7, 8)
    arrived(yd, 7, 8)
    multiply(2, 0)
    multiply(2, 1)
    multiply(2, 3)
    arrived(xu, 6, 7, 8)
    arrived(xd, 6, 7, 8)
    for pair in range(3):
        multiply(pair, 2)
        finish(pair)
    arrived(yu, 9, 10)
    arrived(yd, 9, 10)
    arrived(zs, 6, 7, 8)
    for q in range(4):
        multiply(3, q)
    finish(3)

    for copy in reds:
        copy.wait_recv()
    total = red[0]
    for s in range(1, 8):
        total = total + red[s]
    inner = jnp.sum(total, axis=0, keepdims=True)
    weighted = weight_ref[0] * (diag_ref[...] + inner)
    pol[pole] = jnp.broadcast_to(weighted, pol.shape[1:])
    pols = []
    for d in range(1, n_pole):
        copy = pltpu.make_async_remote_copy(
            src_ref=pol.at[pole],
            dst_ref=pol.at[pole],
            send_sem=pol_send.at[d],
            recv_sem=pol_recv.at[d],
            device_id={"pole": (pole + d) % n_pole},
            device_id_type=MESH,
        )
        copy.start()
        pols.append(copy)
    for copy in pols:
        copy.wait_recv()
    density = pol[0]
    for p in range(1, n_pole):
        density = density + pol[p]
    density_ref[...] = density[:1]

    for copies in (yu, yd, zs, xu, xd, reds, pols):
        for copy in copies:
            copy.wait_send()
    for copy in outs:
        copy.wait()


def per_device(ancestor_inverse, factor_cols, diag_inverse, pole_weights, block_pattern, supernode_ids):
    _, rows, depth = ancestor_inverse.shape
    _, height, width = factor_cols.shape
    blocks = block_pattern.shape[0]
    vmem = pl.BlockSpec(memory_space=pltpu.VMEM)
    anywhere = pl.BlockSpec(memory_space=pl.ANY)
    dma = pltpu.SemaphoreType.DMA
    links = max(len(Y_UP), len(Z_SWAP))
    out, density = pl.pallas_call(
        kernel,
        out_shape=(
            jax.ShapeDtypeStruct((rows, 8 * width), BF16),
            jax.ShapeDtypeStruct((1, width), F32),
        ),
        in_specs=[anywhere, anywhere, vmem, pl.BlockSpec(memory_space=pltpu.SMEM), vmem, vmem],
        out_specs=(anywhere, vmem),
        scratch_shapes=[
            pltpu.VMEM((4, rows, depth), BF16),
            pltpu.VMEM((8, height, width), BF16),
            pltpu.VMEM((4, rows, 2 * width), F32),
            pltpu.VMEM((blocks, width), F32),
            pltpu.VMEM((8, rows, width), BF16),
            pltpu.VMEM((8, 8, width), F32),
            pltpu.VMEM((8, 8, width), F32),
            pltpu.VMEM((8, 8, width), F32),
            dma((5,)),
            dma((8,)),
            dma((3, links)),
            dma((3, links)),
            dma((2, len(X_UP))),
            dma((2, len(X_UP))),
            dma((8,)),
            dma((8,)),
            dma((8,)),
            dma((8,)),
        ],
        compiler_params=pltpu.CompilerParams(
            collective_id=0, has_side_effects=True, vmem_limit_bytes=56 * 1024 * 1024
        ),
        cost_estimate=pl.CostEstimate(
            flops=2 * rows * height * 8 * width, bytes_accessed=6 * 1024 * 1024, transcendentals=0
        ),
    )(
        ancestor_inverse,
        factor_cols,
        diag_inverse,
        pole_weights,
        block_pattern.T,
        supernode_ids.reshape(-1, width),
    )
    return out.reshape(1, rows, 8, 1, width), density.reshape(width)


def solution(mesh):
    in_specs = (
        P("pole", "row", "col"),
        P("pole", None, ("row", "col")),
        P("pole", ("row", "col")),
        P("pole"),
        P(),
        P(),
    )
    out_specs = (P("pole", "row", None, "col", None), P(("row", "col")))
    return jax.shard_map(per_device, mesh=mesh, in_specs=in_specs, out_specs=out_specs, check_vma=False)
```

```python
import functools

import jax
import jax.numpy as jnp
from jax import lax
from jax.experimental import pallas as pl
from jax.experimental.pallas import tpu as pltpu
from jax.sharding import PartitionSpec as P

MESH = pl.DeviceIdType.MESH
F32, BF16 = jnp.float32, jnp.bfloat16

UNITS = 24
OWN, ZP, YN, YP = (0, 0), (0, 1), (1, 0), (3, 0)
YNZ, YPZ, YF, YFZ = (1, 1), (3, 1), (2, 0), (2, 1)
SLOTS = [OWN, ZP, YN, YP, YNZ, YPZ, YF, YFZ]

Y_UP = [
    (OWN, YP, 0, 6), (OWN, YP, 6, 6), (OWN, YP, 14, 10),
    (YP, YF, 0, 6), (YP, YF, 6, 6),
    (ZP, YPZ, 0, 6), (ZP, YPZ, 6, 6), (ZP, YPZ, 12, 2),
    (YPZ, YFZ, 0, 3), (YPZ, YFZ, 3, 3),
    (OWN, YP, 12, 2),
]
Y_DOWN = [
    (OWN, YN, 12, 6), (OWN, YN, 18, 6), (OWN, YN, 0, 10),
    (YN, YF, 12, 6), (YN, YF, 18, 6),
    (ZP, YNZ, 6, 6), (ZP, YNZ, 0, 6), (ZP, YNZ, 12, 2),
    (YNZ, YFZ, 6, 3), (YNZ, YFZ, 9, 3),
    (OWN, YN, 10, 2),
]
Z_SWAP = [
    (OWN, ZP, 0, 6), (OWN, ZP, 6, 6), (OWN, ZP, 12, 6), (OWN, ZP, 18, 4),
    (YN, YNZ, 14, 10), (YP, YPZ, 14, 10),
    (YF, YFZ, 12, 6), (YF, YFZ, 18, 3), (YF, YFZ, 21, 3),
    (OWN, ZP, 22, 2),
]
X_UP = [(0, 3, m) for m in (0, 2, 4, 1, 3, 5)] + [(3, 2, m) for m in (0, 2, 4)]
X_DOWN = [(0, 1, m) for m in (1, 3, 5, 0, 2, 4)] + [(1, 2, m) for m in (1, 3, 5)]
ROUNDS = 4


def at_slot(slot):
    return SLOTS.index(slot)


def kernel(
    a_hbm, f_hbm, diag_ref, weight_ref, pattern_ref, ids_ref,
    out_hbm, density_ref,
    a_all, f_all, acc, coarse, wide, out_vmem, part, red, pol,
    load_sem, out_sem, f_send, f_recv, a_send, a_recv, red_send, red_recv, pol_send, pol_recv, token,
):
    pole, row, col = lax.axis_index("pole"), lax.axis_index("row"), lax.axis_index("col")
    n_pole = lax.axis_size("pole")
    y, z = row // 2, row % 2
    rows, depth = a_all.shape[1], a_all.shape[2]
    unit, sixth, third = f_all.shape[1] // UNITS, rows // 6, rows // 3
    blocks = coarse.shape[0] // 4
    rblk = depth // blocks

    def row_of(slot):
        return ((y + slot[0]) % 4) * 2 + (z + slot[1]) % 2

    x_up, x_down = {"col": (col + 1) % 4}, {"col": (col + 3) % 4}
    y_up, y_down, z_swap = {"row": row_of(YN)}, {"row": row_of(YP)}, {"row": row_of(ZP)}
    z_far = {"pole": (pole + n_pole - 2 + 4 * z) % n_pole, "row": row_of(ZP)}
    core = {"pole": pole + 1 - 2 * (pole % 2)}

    def signal(sem, devices):
        for device in devices:
            pl.semaphore_signal(sem, inc=1, device_id=device, device_id_type=MESH)

    own_rows = pltpu.make_async_copy(a_hbm.at[0], a_all.at[0], load_sem.at[4])
    loads = []
    for q in range(4):
        source = pl.ds(pl.multiple_of(((col + q) % 4) * depth, depth), depth)
        loads.append(
            pltpu.make_async_copy(f_hbm.at[0, source], f_all.at[0, pl.ds(q * depth, depth)], load_sem.at[q])
        )
    for q in (0, 2, 1, 3):
        loads[q].start()

    barrier = pltpu.get_barrier_semaphore()
    friends = [x_up, x_down, y_up, y_down, z_swap, z_far, core]
    signal(barrier, friends)
    own_rows.start()

    def f_copies(link, plan, device):
        copies = []
        for i, (here, there, first, count) in enumerate(plan):
            span = pl.ds(first * unit, count * unit)
            copies.append(
                pltpu.make_async_remote_copy(
                    src_ref=f_all.at[at_slot(here), span],
                    dst_ref=f_all.at[at_slot(there), span],
                    send_sem=f_send.at[link, i],
                    recv_sem=f_recv.at[link, i],
                    device_id=device,
                    device_id_type=MESH,
                )
            )
        return copies

    def a_copies(link, plan, device):
        copies = []
        for i, (here, there, m) in enumerate(plan):
            span = pl.ds(m * sixth, sixth)
            copies.append(
                pltpu.make_async_remote_copy(
                    src_ref=a_hbm.at[0, span] if here == 0 else a_all.at[here, span],
                    dst_ref=a_all.at[there, span],
                    send_sem=a_send.at[link, i],
                    recv_sem=a_recv.at[link, i],
                    device_id=device,
                    device_id_type=MESH,
                )
            )
        return copies

    yu, yd, zs = f_copies(0, Y_UP, y_up), f_copies(1, Y_DOWN, y_down), f_copies(2, Z_SWAP, z_swap)
    xu, xd = a_copies(0, X_UP, x_up), a_copies(1, X_DOWN, x_down)

    def start(copies, *which):
        for i in which:
            copies[i].start()

    def arrived(copies, *which):
        for i in which:
            copies[i].wait_recv()

    ids = ids_ref[pl.ds(row * 4 + col, 1), :]
    onehot = jnp.where(ids == lax.broadcasted_iota(jnp.int32, (pattern_ref.shape[0], ids.shape[1]), 0), 1.0, 0.0)
    coarse[...] = lax.dot_general(
        pattern_ref[...].astype(F32).astype(BF16), onehot.astype(BF16), (((0,), (0,)), ((), ())),
        preferred_element_type=F32,
    )

    def mask_quarter(q):
        loads[q].wait()
        first = ((col + q) % 4) * blocks

        def body(j, carry):
            span = pl.ds(pl.multiple_of(q * depth + j * rblk, rblk), rblk)
            mask = coarse[pl.ds(first + j, 1), :].astype(BF16)
            f_all[0, span, :] = f_all[0, span, :] * mask
            return carry

        lax.fori_loop(0, blocks, body, 0)

    mask_quarter(0)
    pl.semaphore_wait(barrier, len(friends))
    start(xu, 0)
    start(xd, 0)
    start(yu, 0)
    start(zs, 0)
    mask_quarter(2)
    start(yd, 0)
    start(xu, 1)
    start(xd, 1)
    mask_quarter(1)
    start(yu, 1)
    start(zs, 1)
    mask_quarter(3)
    start(yd, 1)
    start(xu, 2)
    start(xd, 2)
    start(yu, 2)
    start(yd, 2)
    start(zs, 2, 3)
    start(xu, 3, 4, 5)
    start(xd, 3, 4, 5)

    def tokens(which):
        signal(token.at[which], [z_swap, z_far, core])
        pl.semaphore_wait(token.at[which], 3)

    begun = set()

    def multiply(slots, first, count, chunks=(0, 1, 2)):
        q = first * unit // depth
        where = slice(chunks[0] * third, (chunks[-1] + 1) * third)
        span = slice(first * unit, (first + count) * unit)
        right = [f_all[at_slot(s), span, :] for s in slots]
        right = right[0] if len(right) == 1 else jnp.concatenate(right, axis=1)
        left = a_all[q, where, first * unit - q * depth : (first + count) * unit - q * depth]
        product = jnp.dot(left, right, preferred_element_type=F32)
        width = product.shape[1] // len(slots)
        for i, slot in enumerate(slots):
            for j, c in enumerate(chunks):
                s, here = at_slot(slot), slice(c * third, (c + 1) * third)
                term = product[j * third : (j + 1) * third, i * width : (i + 1) * width]
                acc[s, here, :] = acc[s, here, :] + term if (slot, c) in begun else term
                begun.add((slot, c))

    own_span = pl.ds(pl.multiple_of(((row * rows // depth - col + 4) % 4) * depth + (row * rows) % depth, rows), rows)
    reds = []

    def reduce_rows(slot):
        s = at_slot(slot)
        terms = f_all[s, own_span, :].astype(F32) * acc[s]
        sums = jnp.sum(terms.reshape(rows // 8, 8, terms.shape[1]), axis=0)
        if slot == OWN:
            red[0] = sums
            return
        part[s] = sums
        back = at_slot(((-slot[0]) % 4, slot[1]))
        copy = pltpu.make_async_remote_copy(
            src_ref=part.at[s],
            dst_ref=red.at[back],
            send_sem=red_send.at[s],
            recv_sem=red_recv.at[back],
            device_id={"row": row_of(slot)},
            device_id_type=MESH,
        )
        copy.start()
        reds.append(copy)

    def place(slot):
        wide[pl.ds(row_of(slot), rows, stride=8), :] = acc[at_slot(slot)]

    own_rows.wait()
    arrived(zs, 0)
    multiply([OWN, ZP], 0, 6)
    arrived(yu, 0, 1)
    start(yu, 3, 4)
    arrived(yd, 0, 1)
    start(yd, 3, 4)
    tokens(0)
    arrived(xu, 0, 1, 2)
    start(xu, 6, 7, 8)
    arrived(xd, 0, 1, 2)
    start(xd, 6, 7, 8)
    tokens(1)
    arrived(zs, 1, 2, 3)
    start(yu, 5, 6, 7)
    start(yd, 5, 6, 7)
    arrived(yu, 2)
    arrived(yd, 2)
    start(zs, 4, 5)
    multiply([YN, YP], 0, 6)
    tokens(2)
    arrived(yu, 3, 4)
    arrived(yd, 3, 4)
    start(zs, 6, 7, 8, 9)
    arrived(xu, 3, 4, 5)
    arrived(xd, 3, 4, 5)
    multiply([OWN, ZP], 6, 6)
    multiply([OWN, ZP], 18, 4)
    multiply([OWN], 22, 2)
    arrived(yu, 5)
    start(yu, 8, 9, 10)
    arrived(yd, 5)
    start(yd, 8, 9, 10)
    tokens(3)
    multiply([YN, YP], 6, 4)
    multiply([YP], 10, 2)
    multiply([YN, YP], 18, 6)
    arrived(xu, 6)
    arrived(xd, 6)
    multiply([OWN, ZP], 12, 6, (0,))
    multiply([YN, YP], 14, 4, (0,))
    multiply([YN], 12, 2, (0,))
    arrived(zs, 4, 5)
    multiply([YNZ, YPZ], 18, 6)
    arrived(yu, 6, 7)
    arrived(yd, 6, 7)
    multiply([YNZ, YPZ], 0, 6)
    multiply([YNZ, YPZ], 6, 6)
    arrived(xu, 7)
    arrived(xd, 7)
    multiply([OWN, ZP], 12, 6, (1,))
    multiply([YN, YP], 14, 4, (1,))
    multiply([YN], 12, 2, (1,))
    multiply([YNZ, YPZ], 12, 6, (0, 1))
    arrived(zs, 6)
    multiply([YF, YFZ], 12, 6, (0, 1))
    arrived(yu, 8)
    multiply([YF, YFZ], 0, 3)
    arrived(yd, 8)
    multiply([YF, YFZ], 6, 3)
    arrived(zs, 7)
    multiply([YF, YFZ], 18, 3)
    arrived(xu, 8)
    arrived(xd, 8)
    multiply([YF, YFZ], 12, 6, (2,))
    multiply([YNZ, YPZ], 12, 6, (2,))
    reduce_rows(YNZ)
    reduce_rows(YPZ)
    arrived(yu, 9)
    multiply([YF, YFZ], 3, 3)
    arrived(yd, 9)
    multiply([YF, YFZ], 9, 3)
    arrived(zs, 8)
    multiply([YF, YFZ], 21, 3)
    reduce_rows(YFZ)
    reduce_rows(YF)
    multiply([OWN, ZP], 12, 6, (2,))
    multiply([YN, YP], 14, 4, (2,))
    multiply([YN], 12, 2, (2,))
    arrived(yu, 10)
    multiply([YP], 12, 2)
    reduce_rows(YP)
    arrived(yd, 10)
    multiply([YN], 10, 2)
    reduce_rows(YN)
    arrived(zs, 9)
    multiply([ZP], 22, 2)
    reduce_rows(ZP)
    reduce_rows(OWN)
    for slot in SLOTS:
        place(slot)

    for copy in reds:
        copy.wait_recv()
    total = red[0]
    for s in range(1, 8):
        total = total + red[s]
    inner = jnp.sum(total, axis=0, keepdims=True)
    weighted = weight_ref[0] * (diag_ref[...] + inner)
    pol[pole] = jnp.broadcast_to(weighted, pol.shape[1:])
    pols = []
    for d in range(1, n_pole):
        copy = pltpu.make_async_remote_copy(
            src_ref=pol.at[pole],
            dst_ref=pol.at[pole],
            send_sem=pol_send.at[d],
            recv_sem=pol_recv.at[d],
            device_id={"pole": (pole + d) % n_pole},
            device_id_type=MESH,
        )
        copy.start()
        pols.append(copy)

    outs = []
    for c in range(3):
        def body(j, carry, c=c):
            base = c * third + j * 32
            block = wide[pl.ds(pl.multiple_of(base * 8, 256), 256), :]
            out_vmem[pl.ds(pl.multiple_of(base, 32), 32)] = (-block).reshape(32, 8, block.shape[1]).astype(BF16)
            return carry

        lax.fori_loop(0, third // 32, body, 0)
        span = pl.ds(c * third, third)
        outs.append(pltpu.make_async_copy(out_vmem.at[span], out_hbm.at[span], out_sem.at[c]))
        outs[-1].start()

    for copy in pols:
        copy.wait_recv()
    density = pol[0]
    for p in range(1, n_pole):
        density = density + pol[p]
    density_ref[...] = density[:1]

    for copies in (yu, yd, zs, xu, xd, reds, pols):
        for copy in copies:
            copy.wait_send()
    for copy in outs:
        copy.wait()


def per_device(ancestor_inverse, factor_cols, diag_inverse, pole_weights, block_pattern, supernode_ids):
    _, rows, depth = ancestor_inverse.shape
    _, height, width = factor_cols.shape
    blocks = block_pattern.shape[0]
    vmem = pl.BlockSpec(memory_space=pltpu.VMEM)
    anywhere = pl.BlockSpec(memory_space=pl.ANY)
    dma = pltpu.SemaphoreType.DMA
    links = max(len(Y_UP), len(Z_SWAP))
    out, density = pl.pallas_call(
        kernel,
        out_shape=(
            jax.ShapeDtypeStruct((rows, 8, width), BF16),
            jax.ShapeDtypeStruct((1, width), F32),
        ),
        in_specs=[anywhere, anywhere, vmem, pl.BlockSpec(memory_space=pltpu.SMEM), vmem, vmem],
        out_specs=(anywhere, vmem),
        scratch_shapes=[
            pltpu.VMEM((4, rows, depth), BF16),
            pltpu.VMEM((8, height, width), BF16),
            pltpu.VMEM((8, rows, width), F32),
            pltpu.VMEM((blocks, width), F32),
            pltpu.VMEM((rows * 8, width), F32),
            pltpu.VMEM((rows, 8, width), BF16),
            pltpu.VMEM((8, 8, width), F32),
            pltpu.VMEM((8, 8, width), F32),
            pltpu.VMEM((8, 8, width), F32),
            dma((5,)),
            dma((8,)),
            dma((3, links)),
            dma((3, links)),
            dma((2, len(X_UP))),
            dma((2, len(X_UP))),
            dma((8,)),
            dma((8,)),
            dma((8,)),
            dma((8,)),
            pltpu.SemaphoreType.REGULAR((ROUNDS,)),
        ],
        compiler_params=pltpu.CompilerParams(
            collective_id=0, has_side_effects=True, vmem_limit_bytes=56 * 1024 * 1024
        ),
        cost_estimate=pl.CostEstimate(
            flops=2 * rows * height * 8 * width, bytes_accessed=6 * 1024 * 1024, transcendentals=0
        ),
    )(
        ancestor_inverse,
        factor_cols,
        diag_inverse,
        pole_weights,
        block_pattern.T,
        supernode_ids.reshape(-1, width),
    )
    return out.reshape(1, rows, 8, 1, width), density.reshape(width)


def solution(mesh):
    in_specs = (
        P("pole", "row", "col"),
        P("pole", None, ("row", "col")),
        P("pole", ("row", "col")),
        P("pole"),
        P(),
        P(),
    )
    out_specs = (P("pole", "row", None, "col", None), P(("row", "col")))
    return jax.shard_map(per_device, mesh=mesh, in_specs=in_specs, out_specs=out_specs, check_vma=False)
```

```python
import functools

import jax
import jax.numpy as jnp
from jax import lax
from jax.experimental import pallas as pl
from jax.experimental.pallas import tpu as pltpu
from jax.sharding import PartitionSpec as P

MESH = pl.DeviceIdType.MESH
F32, BF16 = jnp.float32, jnp.bfloat16

UNITS = 24
OWN, ZP, YN, YP = (0, 0), (0, 1), (1, 0), (3, 0)
YNZ, YPZ, YF, YFZ = (1, 1), (3, 1), (2, 0), (2, 1)
SLOTS = [OWN, ZP, YN, YP, YNZ, YPZ, YF, YFZ]

Y_UP = [
    (OWN, YP, 0, 6), (OWN, YP, 6, 6), (OWN, YP, 16, 8),
    (YP, YF, 0, 6), (YP, YF, 6, 6),
    (ZP, YPZ, 0, 6), (ZP, YPZ, 6, 4), (ZP, YPZ, 12, 4),
    (YPZ, YFZ, 0, 6),
    (OWN, YP, 12, 2), (OWN, YP, 14, 2),
]
Y_DOWN = [
    (OWN, YN, 12, 6), (OWN, YN, 18, 6), (OWN, YN, 0, 8),
    (YN, YF, 12, 6), (YN, YF, 18, 6),
    (ZP, YNZ, 6, 6), (ZP, YNZ, 0, 6), (ZP, YNZ, 12, 2),
    (YNZ, YFZ, 6, 6),
    (OWN, YN, 8, 2), (OWN, YN, 10, 2),
]
Z_SWAP = [
    (OWN, ZP, 0, 6), (OWN, ZP, 6, 6), (OWN, ZP, 12, 6), (OWN, ZP, 18, 2),
    (YN, YNZ, 14, 10), (YP, YPZ, 16, 8), (YP, YPZ, 10, 2),
    (YF, YFZ, 12, 6), (YF, YFZ, 18, 6),
    (OWN, ZP, 20, 2), (OWN, ZP, 22, 2),
]
X_UP = [(0, 3, m) for m in (0, 2, 4, 1, 3, 5)] + [(3, 2, m) for m in (0, 2, 4)]
X_DOWN = [(0, 1, m) for m in (1, 3, 5, 0, 2, 4)] + [(1, 2, m) for m in (1, 3, 5)]
ROUNDS = 4


def at_slot(slot):
    return SLOTS.index(slot)


def kernel(
    a_hbm, f_hbm, diag_hbm, weight_ref, pattern_hbm, ids_hbm,
    out_ref, density_ref,
    a_all, f_all, acc, coarse, wide, diag_ref, pattern_ref, ids_ref, part, red, pol,
    load_sem, f_send, f_recv, a_send, a_recv, red_send, red_recv, pol_send, pol_recv, token,
):
    pole, row, col = lax.axis_index("pole"), lax.axis_index("row"), lax.axis_index("col")
    n_pole = lax.axis_size("pole")
    y, z = row // 2, row % 2
    rows, depth = a_all.shape[1], a_all.shape[2]
    unit, sixth, third = f_all.shape[1] // UNITS, rows // 6, rows // 3
    blocks = coarse.shape[0] // 4
    rblk = depth // blocks

    def row_of(slot):
        return ((y + slot[0]) % 4) * 2 + (z + slot[1]) % 2

    x_up, x_down = {"col": (col + 1) % 4}, {"col": (col + 3) % 4}
    y_up, y_down, z_swap = {"row": row_of(YN)}, {"row": row_of(YP)}, {"row": row_of(ZP)}
    z_far = {"pole": (pole + n_pole - 2 + 4 * z) % n_pole, "row": row_of(ZP)}
    core = {"pole": pole + 1 - 2 * (pole % 2)}

    def signal(sem, devices):
        for device in devices:
            pl.semaphore_signal(sem, inc=1, device_id=device, device_id_type=MESH)

    own_rows = pltpu.make_async_copy(a_hbm.at[0], a_all.at[0], load_sem.at[4])
    loads = []
    for q in range(4):
        source = pl.ds(pl.multiple_of(((col + q) % 4) * depth, depth), depth)
        loads.append(
            pltpu.make_async_copy(f_hbm.at[0, source], f_all.at[0, pl.ds(q * depth, depth)], load_sem.at[q])
        )
    small = [
        pltpu.make_async_copy(source, target, load_sem.at[5 + i])
        for i, (source, target) in enumerate([(ids_hbm, ids_ref), (pattern_hbm, pattern_ref), (diag_hbm, diag_ref)])
    ]

    barrier = pltpu.get_barrier_semaphore()
    friends = [x_up, x_down, y_up, y_down, z_swap, z_far, core]
    signal(barrier, friends)
    for copy in small:
        copy.start()
    for q in (0, 2, 1, 3):
        loads[q].start()
    own_rows.start()

    def f_copies(link, plan, device):
        copies = []
        for i, (here, there, first, count) in enumerate(plan):
            span = pl.ds(first * unit, count * unit)
            copies.append(
                pltpu.make_async_remote_copy(
                    src_ref=f_all.at[at_slot(here), span],
                    dst_ref=f_all.at[at_slot(there), span],
                    send_sem=f_send.at[link, i],
                    recv_sem=f_recv.at[link, i],
                    device_id=device,
                    device_id_type=MESH,
                )
            )
        return copies

    def a_copies(link, plan, device):
        copies = []
        for i, (here, there, m) in enumerate(plan):
            span = pl.ds(m * sixth, sixth)
            copies.append(
                pltpu.make_async_remote_copy(
                    src_ref=a_hbm.at[0, span] if here == 0 else a_all.at[here, span],
                    dst_ref=a_all.at[there, span],
                    send_sem=a_send.at[link, i],
                    recv_sem=a_recv.at[link, i],
                    device_id=device,
                    device_id_type=MESH,
                )
            )
        return copies

    yu, yd, zs = f_copies(0, Y_UP, y_up), f_copies(1, Y_DOWN, y_down), f_copies(2, Z_SWAP, z_swap)
    xu, xd = a_copies(0, X_UP, x_up), a_copies(1, X_DOWN, x_down)

    def start(copies, *which):
        for i in which:
            copies[i].start()

    def arrived(copies, *which):
        for i in which:
            copies[i].wait_recv()

    for copy in small:
        copy.wait()
    ids = ids_ref[pl.ds(row * 4 + col, 1), :]
    onehot = jnp.where(ids == lax.broadcasted_iota(jnp.int32, (pattern_ref.shape[0], ids.shape[1]), 0), 1.0, 0.0)
    coarse[...] = lax.dot_general(
        pattern_ref[...].astype(F32).astype(BF16), onehot.astype(BF16), (((0,), (0,)), ((), ())),
        preferred_element_type=F32,
    )

    def mask_quarter(q):
        loads[q].wait()
        first = ((col + q) % 4) * blocks

        def body(j, carry):
            span = pl.ds(pl.multiple_of(q * depth + j * rblk, rblk), rblk)
            mask = coarse[pl.ds(first + j, 1), :].astype(BF16)
            f_all[0, span, :] = f_all[0, span, :] * mask
            return carry

        lax.fori_loop(0, blocks, body, 0)

    mask_quarter(0)
    pl.semaphore_wait(barrier, len(friends))
    start(xu, 0)
    start(xd, 0)
    start(yu, 0)
    start(zs, 0)
    mask_quarter(2)
    start(yd, 0)
    start(xu, 1)
    start(xd, 1)
    mask_quarter(1)
    start(yu, 1)
    start(zs, 1)
    mask_quarter(3)
    start(yd, 1)
    start(xu, 2)
    start(xd, 2)
    start(yu, 2)
    start(yd, 2)
    start(zs, 2, 3)
    start(xu, 3, 4, 5)
    start(xd, 3, 4, 5)

    def tokens(which):
        signal(token.at[which], [z_swap, z_far, core])
        pl.semaphore_wait(token.at[which], 3)

    begun = set()

    def multiply(slots, first, count, chunks=(0, 1, 2)):
        q = first * unit // depth
        where = slice(chunks[0] * third, (chunks[-1] + 1) * third)
        span = slice(first * unit, (first + count) * unit)
        right = [f_all[at_slot(s), span, :] for s in slots]
        right = right[0] if len(right) == 1 else jnp.concatenate(right, axis=1)
        left = a_all[q, where, first * unit - q * depth : (first + count) * unit - q * depth]
        product = jnp.dot(left, right, preferred_element_type=F32)
        width = product.shape[1] // len(slots)
        for i, slot in enumerate(slots):
            for j, c in enumerate(chunks):
                s, here = at_slot(slot), slice(c * third, (c + 1) * third)
                term = product[j * third : (j + 1) * third, i * width : (i + 1) * width]
                acc[s, here, :] = acc[s, here, :] + term if (slot, c) in begun else term
                begun.add((slot, c))

    own_span = pl.ds(pl.multiple_of(((row * rows // depth - col + 4) % 4) * depth + (row * rows) % depth, rows), rows)
    reds = []

    def reduce_rows(slot):
        s = at_slot(slot)
        terms = f_all[s, own_span, :].astype(F32) * acc[s]
        sums = jnp.sum(terms.reshape(rows // 8, 8, terms.shape[1]), axis=0)
        if slot == OWN:
            red[0] = sums
            return
        part[s] = sums
        back = at_slot(((-slot[0]) % 4, slot[1]))
        copy = pltpu.make_async_remote_copy(
            src_ref=part.at[s],
            dst_ref=red.at[back],
            send_sem=red_send.at[s],
            recv_sem=red_recv.at[back],
            device_id={"row": row_of(slot)},
            device_id_type=MESH,
        )
        copy.start()
        reds.append(copy)

    def place(slot):
        wide[pl.ds(row_of(slot), rows, stride=8), :] = acc[at_slot(slot)]

    own_rows.wait()
    arrived(zs, 0)
    multiply([OWN, ZP], 0, 6)
    arrived(yu, 0, 1)
    start(yu, 3, 4)
    arrived(yd, 0, 1)
    start(yd, 3, 4)
    start(zs, 4)
    tokens(0)
    arrived(xu, 0, 1, 2)
    start(xu, 6, 7, 8)
    arrived(xd, 0, 1, 2)
    start(xd, 6, 7, 8)
    tokens(1)
    arrived(zs, 1, 2, 3)
    start(yu, 5, 6, 7)
    start(yd, 5, 6, 7)
    arrived(yu, 2)
    start(zs, 5, 6)
    arrived(yd, 2)
    multiply([YN, YP], 0, 6)
    tokens(2)
    arrived(yu, 3, 4)
    arrived(yd, 3, 4)
    start(zs, 7, 8, 9, 10)
    arrived(xu, 3, 4, 5)
    arrived(xd, 3, 4, 5)
    multiply([OWN, ZP], 6, 6)
    multiply([OWN, ZP], 18, 2)
    multiply([OWN], 20, 4)
    arrived(yu, 5)
    start(yu, 8, 9, 10)
    arrived(yd, 5)
    start(yd, 8, 9, 10)
    tokens(3)
    multiply([YN, YP], 6, 2)
    multiply([YP], 8, 4)
    multiply([YN, YP], 18, 6)
    arrived(zs, 4, 5, 6)
    multiply([YNZ, YPZ], 18, 6)
    arrived(xu, 6)
    arrived(xd, 6)
    multiply([OWN, ZP], 12, 6, (0,))
    multiply([YN, YP], 16, 2, (0,))
    multiply([YN], 12, 4, (0,))
    arrived(yu, 6)
    multiply([YNZ, YPZ], 6, 6)
    arrived(yd, 6)
    multiply([YNZ, YPZ], 0, 6)
    arrived(yu, 7)
    arrived(yd, 7)
    multiply([YNZ, YPZ], 12, 6, (0,))
    arrived(zs, 7)
    multiply([YF, YFZ], 12, 6, (0,))
    arrived(xu, 7)
    arrived(xd, 7)
    multiply([OWN, ZP], 12, 6, (1,))
    multiply([YN, YP], 16, 2, (1,))
    multiply([YN], 12, 4, (1,))
    multiply([YNZ, YPZ], 12, 6, (1,))
    multiply([YF, YFZ], 12, 6, (1,))
    arrived(yu, 8)
    multiply([YF, YFZ], 0, 6)
    arrived(yd, 8)
    multiply([YF, YFZ], 6, 6)
    arrived(zs, 8)
    multiply([YF, YFZ], 18, 6)
    arrived(xu, 8)
    arrived(xd, 8)
    multiply([YF, YFZ], 12, 6, (2,))
    reduce_rows(YFZ)
    reduce_rows(YF)
    multiply([YNZ, YPZ], 12, 6, (2,))
    reduce_rows(YNZ)
    reduce_rows(YPZ)
    multiply([OWN, ZP], 12, 6, (2,))
    multiply([YN, YP], 16, 2, (2,))
    multiply([YN], 12, 4, (2,))
    arrived(yu, 9)
    multiply([YP], 12, 2)
    arrived(yd, 9)
    multiply([YN], 8, 2)
    arrived(zs, 9)
    multiply([ZP], 20, 2)
    reduce_rows(OWN)
    arrived(yu, 10)
    multiply([YP], 14, 2)
    reduce_rows(YP)
    arrived(yd, 10)
    multiply([YN], 10, 2)
    reduce_rows(YN)
    arrived(zs, 10)
    multiply([ZP], 22, 2)
    reduce_rows(ZP)

    for copy in reds:
        copy.wait_recv()
    total = red[0]
    for s in range(1, 8):
        total = total + red[s]
    inner = jnp.sum(total, axis=0, keepdims=True)
    weighted = weight_ref[0] * (diag_ref[...] + inner)
    pol[pole] = jnp.broadcast_to(weighted, pol.shape[1:])
    pols = []
    for d in sorted(range(1, n_pole), key=lambda d: abs(d - n_pole // 2)):
        copy = pltpu.make_async_remote_copy(
            src_ref=pol.at[pole],
            dst_ref=pol.at[pole],
            send_sem=pol_send.at[d],
            recv_sem=pol_recv.at[d],
            device_id={"pole": (pole + d) % n_pole},
            device_id_type=MESH,
        )
        copy.start()
        pols.append(copy)

    for slot in SLOTS:
        place(slot)

    def body(j, carry):
        base = pl.multiple_of(j * 32, 32)
        block = wide[pl.ds(pl.multiple_of(base * 8, 256), 256), :]
        out_ref[pl.ds(base, 32)] = (-block).reshape(32, 8, block.shape[1]).astype(BF16)
        return carry

    lax.fori_loop(0, rows // 32, body, 0)

    for copy in pols:
        copy.wait_recv()
    density = pol[0]
    for p in range(1, n_pole):
        density = density + pol[p]
    density_ref[...] = density[:1]

    for copies in (yu, yd, zs, xu, xd, reds, pols):
        for copy in copies:
            copy.wait_send()


def per_device(ancestor_inverse, factor_cols, diag_inverse, pole_weights, block_pattern, supernode_ids):
    _, rows, depth = ancestor_inverse.shape
    _, height, width = factor_cols.shape
    blocks = block_pattern.shape[0]
    vmem = pl.BlockSpec(memory_space=pltpu.VMEM)
    anywhere = pl.BlockSpec(memory_space=pl.ANY)
    dma = pltpu.SemaphoreType.DMA
    links = max(len(Y_UP), len(Z_SWAP))
    out, density = pl.pallas_call(
        kernel,
        out_shape=(
            pltpu.VMEM((rows, 8, width), BF16),
            pltpu.VMEM((1, width), F32),
        ),
        in_specs=[anywhere, anywhere, anywhere, pl.BlockSpec(memory_space=pltpu.SMEM), anywhere, anywhere],
        out_specs=(vmem, vmem),
        scratch_shapes=[
            pltpu.VMEM((4, rows, depth), BF16),
            pltpu.VMEM((8, height, width), BF16),
            pltpu.VMEM((8, rows, width), F32),
            pltpu.VMEM((blocks, width), F32),
            pltpu.VMEM((rows * 8, width), F32),
            pltpu.VMEM((1, width), F32),
            pltpu.VMEM(block_pattern.shape[::-1], jnp.int32),
            pltpu.VMEM((supernode_ids.size // width, width), jnp.int32),
            pltpu.VMEM((8, 8, width), F32),
            pltpu.VMEM((8, 8, width), F32),
            pltpu.VMEM((8, 8, width), F32),
            dma((8,)),
            dma((3, links)),
            dma((3, links)),
            dma((2, len(X_UP))),
            dma((2, len(X_UP))),
            dma((8,)),
            dma((8,)),
            dma((8,)),
            dma((8,)),
            pltpu.SemaphoreType.REGULAR((ROUNDS,)),
        ],
        compiler_params=pltpu.CompilerParams(
            collective_id=0, has_side_effects=True, vmem_limit_bytes=63_400_000
        ),
        cost_estimate=pl.CostEstimate(
            flops=2 * rows * height * 8 * width, bytes_accessed=6 * 1024 * 1024, transcendentals=0
        ),
    )(
        ancestor_inverse,
        factor_cols,
        diag_inverse,
        pole_weights,
        block_pattern.T,
        supernode_ids.reshape(-1, width),
    )
    return out.reshape(1, rows, 8, 1, width), density.reshape(width)


def solution(mesh):
    in_specs = (
        P("pole", "row", "col"),
        P("pole", None, ("row", "col")),
        P("pole", ("row", "col")),
        P("pole"),
        P(),
        P(),
    )
    out_specs = (P("pole", "row", None, "col", None), P(("row", "col")))
    return jax.shard_map(per_device, mesh=mesh, in_specs=in_specs, out_specs=out_specs, check_vma=False)
```

```python
import functools

import jax
import jax.numpy as jnp
from jax import lax
from jax.experimental import pallas as pl
from jax.experimental.pallas import tpu as pltpu
from jax.sharding import PartitionSpec as P

MESH = pl.DeviceIdType.MESH
F32, BF16 = jnp.float32, jnp.bfloat16

UNITS = 24
OWN, ZP, YN, YP = (0, 0), (0, 1), (1, 0), (3, 0)
YNZ, YPZ, YF, YFZ = (1, 1), (3, 1), (2, 0), (2, 1)
SLOTS = [OWN, ZP, YN, YP, YNZ, YPZ, YF, YFZ]

Y_UP = [
    (OWN, YP, 0, 6), (OWN, YP, 18, 6), (OWN, YP, 12, 6), (OWN, YP, 6, 2),
    (YP, YF, 0, 6), (YP, YF, 18, 6),
    (ZP, YPZ, 0, 6), (ZP, YPZ, 6, 6), (ZP, YPZ, 12, 2),
    (YPZ, YFZ, 0, 6),
    (OWN, YP, 8, 3), (OWN, YP, 11, 1),
]
Y_DOWN = [
    (OWN, YN, 12, 6), (OWN, YN, 18, 6), (OWN, YN, 6, 6), (OWN, YN, 0, 2),
    (YN, YF, 12, 6), (YN, YF, 6, 6),
    (ZP, YNZ, 6, 6), (ZP, YNZ, 0, 6), (ZP, YNZ, 12, 2),
    (YNZ, YFZ, 6, 6),
    (OWN, YN, 2, 3), (OWN, YN, 5, 1),
]
Z_SWAP = [
    (OWN, ZP, 0, 6), (OWN, ZP, 6, 6), (OWN, ZP, 12, 8),
    (YN, YNZ, 14, 10), (YP, YPZ, 14, 10),
    (YF, YFZ, 12, 6), (YF, YFZ, 18, 6),
    (OWN, ZP, 20, 3), (OWN, ZP, 23, 1),
]
HALVES = [[(0, 10), (20, 10), (40, 4)], [(10, 10), (30, 10), (44, 4)]]
X_UP = [(0, 3, *m) for m in HALVES[0] + HALVES[1]] + [(3, 2, *m) for m in HALVES[0]]
X_DOWN = [(0, 1, *m) for m in HALVES[1] + HALVES[0]] + [(1, 2, *m) for m in HALVES[1]]
CHUNKS = [(0, 20), (20, 40), (40, 48)]
ROUNDS = 4


def at_slot(slot):
    return SLOTS.index(slot)


def kernel(
    a_hbm, f_hbm, diag_hbm, weight_ref, pattern_hbm, ids_hbm,
    out_ref, density_ref,
    a_all, f_all, acc, coarse, wide, diag_ref, pattern_ref, ids_ref, part, red, pol,
    load_sem, f_send, f_recv, a_send, a_recv, red_send, red_recv, pol_send, pol_recv, token,
):
    pole, row, col = lax.axis_index("pole"), lax.axis_index("row"), lax.axis_index("col")
    n_pole = lax.axis_size("pole")
    y, z = row // 2, row % 2
    rows, depth = a_all.shape[1], a_all.shape[2]
    unit, part_rows = f_all.shape[1] // UNITS, rows // 48
    blocks = coarse.shape[0] // 4
    rblk = depth // blocks

    def row_of(slot):
        return ((y + slot[0]) % 4) * 2 + (z + slot[1]) % 2

    x_up, x_down = {"col": (col + 1) % 4}, {"col": (col + 3) % 4}
    y_up, y_down, z_swap = {"row": row_of(YN)}, {"row": row_of(YP)}, {"row": row_of(ZP)}
    z_far = {"pole": (pole + n_pole - 2 + 4 * z) % n_pole, "row": row_of(ZP)}
    core = {"pole": pole + 1 - 2 * (pole % 2)}

    def signal(sem, devices):
        for device in devices:
            pl.semaphore_signal(sem, inc=1, device_id=device, device_id_type=MESH)

    own_rows = pltpu.make_async_copy(a_hbm.at[0], a_all.at[0], load_sem.at[4])
    loads = []
    for q in range(4):
        source = pl.ds(pl.multiple_of(((col + q) % 4) * depth, depth), depth)
        loads.append(
            pltpu.make_async_copy(f_hbm.at[0, source], f_all.at[0, pl.ds(q * depth, depth)], load_sem.at[q])
        )
    small = [
        pltpu.make_async_copy(source, target, load_sem.at[5 + i])
        for i, (source, target) in enumerate([(ids_hbm, ids_ref), (pattern_hbm, pattern_ref), (diag_hbm, diag_ref)])
    ]

    barrier = pltpu.get_barrier_semaphore()
    friends = [x_up, x_down, y_up, y_down, z_swap, z_far, core]
    signal(barrier, friends)
    for copy in small:
        copy.start()
    for q in (0, 2, 1, 3):
        loads[q].start()
    own_rows.start()

    def f_copies(link, plan, device):
        copies = []
        for i, (here, there, first, count) in enumerate(plan):
            span = pl.ds(first * unit, count * unit)
            copies.append(
                pltpu.make_async_remote_copy(
                    src_ref=f_all.at[at_slot(here), span],
                    dst_ref=f_all.at[at_slot(there), span],
                    send_sem=f_send.at[link, i],
                    recv_sem=f_recv.at[link, i],
                    device_id=device,
                    device_id_type=MESH,
                )
            )
        return copies

    def a_copies(link, plan, device):
        copies = []
        for i, (here, there, first, count) in enumerate(plan):
            span = pl.ds(first * part_rows, count * part_rows)
            copies.append(
                pltpu.make_async_remote_copy(
                    src_ref=a_hbm.at[0, span] if here == 0 else a_all.at[here, span],
                    dst_ref=a_all.at[there, span],
                    send_sem=a_send.at[link, i],
                    recv_sem=a_recv.at[link, i],
                    device_id=device,
                    device_id_type=MESH,
                )
            )
        return copies

    yu, yd, zs = f_copies(0, Y_UP, y_up), f_copies(1, Y_DOWN, y_down), f_copies(2, Z_SWAP, z_swap)
    xu, xd = a_copies(0, X_UP, x_up), a_copies(1, X_DOWN, x_down)

    def start(copies, *which):
        for i in which:
            copies[i].start()

    def arrived(copies, *which):
        for i in which:
            copies[i].wait_recv()

    for copy in small:
        copy.wait()
    ids = ids_ref[pl.ds(row * 4 + col, 1), :]
    onehot = jnp.where(ids == lax.broadcasted_iota(jnp.int32, (pattern_ref.shape[0], ids.shape[1]), 0), 1.0, 0.0)
    coarse[...] = lax.dot_general(
        pattern_ref[...].astype(F32).astype(BF16), onehot.astype(BF16), (((0,), (0,)), ((), ())),
        preferred_element_type=F32,
    )

    def mask_quarter(q):
        loads[q].wait()
        first = ((col + q) % 4) * blocks

        def body(j, carry):
            span = pl.ds(pl.multiple_of(q * depth + j * rblk, rblk), rblk)
            mask = coarse[pl.ds(first + j, 1), :].astype(BF16)
            f_all[0, span, :] = f_all[0, span, :] * mask
            return carry

        lax.fori_loop(0, blocks, body, 0)

    mask_quarter(0)
    pl.semaphore_wait(barrier, len(friends))
    start(yu, 0)
    start(zs, 0)
    start(xu, 0)
    start(xd, 0)
    mask_quarter(2)
    start(yd, 0)
    mask_quarter(1)
    start(zs, 1)
    mask_quarter(3)
    start(yu, 1)
    start(yd, 1)
    start(yd, 2)
    start(xu, 1)
    start(xd, 1)
    start(yu, 2)
    start(zs, 2)
    start(yu, 3)
    start(yd, 3)
    start(xu, 2, 3, 4, 5)
    start(xd, 2, 3, 4, 5)

    def tokens(which):
        signal(token.at[which], [z_swap, z_far, core])
        pl.semaphore_wait(token.at[which], 3)

    begun = set()

    def product_of(slots, first, count, where):
        q = first * unit // depth
        span = slice(first * unit, (first + count) * unit)
        right = [f_all[at_slot(s), span, :] for s in slots]
        right = right[0] if len(right) == 1 else jnp.concatenate(right, axis=1)
        left = a_all[q, where, first * unit - q * depth : (first + count) * unit - q * depth]
        return jnp.dot(left, right, preferred_element_type=F32)

    def multiply(slots, first, count, chunks=(0, 1, 2)):
        base = CHUNKS[chunks[0]][0] * part_rows
        product = product_of(slots, first, count, slice(base, CHUNKS[chunks[-1]][1] * part_rows))
        width = product.shape[1] // len(slots)
        for i, slot in enumerate(slots):
            for c in chunks:
                s, begin, end = at_slot(slot), CHUNKS[c][0] * part_rows, CHUNKS[c][1] * part_rows
                term = product[begin - base : end - base, i * width : (i + 1) * width]
                acc[s, begin:end, :] = acc[s, begin:end, :] + term if (slot, c) in begun else term
                begun.add((slot, c))

    own_span = pl.ds(pl.multiple_of(((row * rows // depth - col + 4) % 4) * depth + (row * rows) % depth, rows), rows)
    reds = []

    def place(slot, total):
        wide[pl.ds(row_of(slot), rows, stride=8), :] = total

    def finish(pieces):
        totals = [acc[at_slot(slot)] + product_of([slot], first, count, slice(0, rows)) for slot, first, count in pieces]
        for (slot, _, _), total in zip(pieces, totals):
            reduce_rows(slot, total)
        for (slot, _, _), total in zip(pieces, totals):
            place(slot, total)

    def reduce_rows(slot, total):
        s = at_slot(slot)
        terms = f_all[s, own_span, :].astype(F32) * total
        sums = jnp.sum(terms.reshape(rows // 8, 8, terms.shape[1]), axis=0)
        if slot == OWN:
            red[0] = sums
            return
        part[s] = sums
        back = at_slot(((-slot[0]) % 4, slot[1]))
        copy = pltpu.make_async_remote_copy(
            src_ref=part.at[s],
            dst_ref=red.at[back],
            send_sem=red_send.at[s],
            recv_sem=red_recv.at[back],
            device_id={"row": row_of(slot)},
            device_id_type=MESH,
        )
        copy.start()
        reds.append(copy)

    own_rows.wait()
    arrived(zs, 0)
    multiply([OWN, ZP], 0, 6)
    arrived(yu, 0, 1)
    start(yu, 4, 5)
    arrived(yd, 0, 1)
    start(zs, 3)
    start(yd, 4)
    tokens(0)
    arrived(yd, 2)
    start(yd, 5)
    arrived(xu, 0, 1, 2)
    start(xu, 6, 7, 8)
    arrived(xd, 0, 1, 2)
    start(xd, 6, 7, 8)
    arrived(zs, 1, 2)
    start(yu, 6, 7, 8)
    start(yd, 6, 7, 8)
    arrived(yu, 2)
    start(zs, 4)
    tokens(1)
    arrived(yu, 3)
    arrived(yd, 3)
    multiply([YN, YP], 0, 2)
    multiply([YP], 2, 4)
    tokens(2)
    arrived(yu, 4, 5)
    arrived(yd, 4, 5)
    start(zs, 5, 6, 7, 8)
    tokens(3)
    arrived(xu, 3, 4, 5)
    arrived(xd, 3, 4, 5)
    multiply([OWN, ZP], 6, 6)
    multiply([OWN, ZP], 18, 2)
    multiply([OWN], 20, 4)
    arrived(yu, 6)
    start(yu, 9, 10, 11)
    arrived(yd, 6)
    start(yd, 9, 10, 11)
    multiply([YN, YP], 6, 2)
    multiply([YN], 8, 4)
    multiply([YN, YP], 18, 6)
    arrived(zs, 3, 4)
    multiply([YNZ, YPZ], 18, 6)
    arrived(yu, 7)
    arrived(yd, 7)
    multiply([YNZ, YPZ], 0, 6)
    multiply([YNZ, YPZ], 6, 6)
    arrived(xu, 6)
    arrived(xd, 6)
    multiply([OWN, ZP, YN, YP], 12, 6, (0,))
    arrived(yu, 8)
    arrived(yd, 8)
    arrived(zs, 5)
    multiply([YNZ, YPZ, YF, YFZ], 12, 6, (0,))
    arrived(xu, 7)
    arrived(xd, 7)
    multiply(SLOTS, 12, 6, (1,))
    arrived(yu, 9)
    multiply([YF, YFZ], 0, 6)
    arrived(yd, 9)
    multiply([YF, YFZ], 6, 6)
    arrived(zs, 6)
    multiply([YF, YFZ], 18, 6)
    arrived(xu, 8)
    arrived(xd, 8)
    multiply(SLOTS, 12, 6, (2,))
    for slot in (YFZ, YF, YNZ, YPZ, OWN):
        reduce_rows(slot, acc[at_slot(slot)])
    arrived(yu, 10)
    arrived(yd, 10)
    arrived(zs, 7)
    multiply([YP], 8, 3)
    multiply([YN], 2, 3)
    multiply([ZP], 20, 3)
    arrived(yu, 11)
    arrived(yd, 11)
    arrived(zs, 8)
    finish([(YP, 11, 1), (YN, 5, 1), (ZP, 23, 1)])

    for copy in reds:
        copy.wait_recv()
    total = red[0]
    for s in range(1, 8):
        total = total + red[s]
    inner = jnp.sum(total, axis=0, keepdims=True)
    weighted = weight_ref[0] * (diag_ref[...] + inner)
    pol[pole] = jnp.broadcast_to(weighted, pol.shape[1:])
    pols = []
    for d in sorted(range(1, n_pole), key=lambda d: abs(d - n_pole // 2)):
        copy = pltpu.make_async_remote_copy(
            src_ref=pol.at[pole],
            dst_ref=pol.at[pole],
            send_sem=pol_send.at[d],
            recv_sem=pol_recv.at[d],
            device_id={"pole": (pole + d) % n_pole},
            device_id_type=MESH,
        )
        copy.start()
        pols.append(copy)

    for slot in (OWN, YNZ, YPZ, YF, YFZ):
        place(slot, acc[at_slot(slot)])

    def body(j, carry):
        base = pl.multiple_of(j * 32, 32)
        block = wide[pl.ds(pl.multiple_of(base * 8, 256), 256), :]
        out_ref[pl.ds(base, 32)] = (-block).reshape(32, 8, block.shape[1]).astype(BF16)
        return carry

    lax.fori_loop(0, rows // 32, body, 0)

    for copy in pols:
        copy.wait_recv()
    density = pol[0]
    for p in range(1, n_pole):
        density = density + pol[p]
    density_ref[...] = density[:1]

    for copies in (yu, yd, zs, xu, xd, reds, pols):
        for copy in copies:
            copy.wait_send()


def hand_over(out_ref, density_ref, out_hbm, density_hbm, sems):
    rows = out_ref.shape[0]
    copies = [pltpu.make_async_copy(density_ref, density_hbm, sems.at[4])]
    for i in range(4):
        span = pl.ds(i * (rows // 4), rows // 4)
        copies.append(pltpu.make_async_copy(out_ref.at[span], out_hbm.at[span], sems.at[i]))
    for copy in copies:
        copy.start()
    for copy in copies:
        copy.wait()


def per_device(ancestor_inverse, factor_cols, diag_inverse, pole_weights, block_pattern, supernode_ids):
    _, rows, depth = ancestor_inverse.shape
    _, height, width = factor_cols.shape
    blocks = block_pattern.shape[0]
    vmem = pl.BlockSpec(memory_space=pltpu.VMEM)
    anywhere = pl.BlockSpec(memory_space=pl.ANY)
    dma = pltpu.SemaphoreType.DMA
    links = max(len(Y_UP), len(Z_SWAP))
    out, density = pl.pallas_call(
        kernel,
        out_shape=(
            pltpu.VMEM((rows, 8, width), BF16),
            pltpu.VMEM((1, width), F32),
        ),
        in_specs=[anywhere, anywhere, anywhere, pl.BlockSpec(memory_space=pltpu.SMEM), anywhere, anywhere],
        out_specs=(vmem, vmem),
        scratch_shapes=[
            pltpu.VMEM((4, rows, depth), BF16),
            pltpu.VMEM((8, height, width), BF16),
            pltpu.VMEM((8, rows, width), F32),
            pltpu.VMEM((blocks, width), F32),
            pltpu.VMEM((rows * 8, width), F32),
            pltpu.VMEM((1, width), F32),
            pltpu.VMEM(block_pattern.shape[::-1], jnp.int32),
            pltpu.VMEM((supernode_ids.size // width, width), jnp.int32),
            pltpu.VMEM((8, 8, width), F32),
            pltpu.VMEM((8, 8, width), F32),
            pltpu.VMEM((8, 8, width), F32),
            dma((8,)),
            dma((3, links)),
            dma((3, links)),
            dma((2, len(X_UP))),
            dma((2, len(X_UP))),
            dma((8,)),
            dma((8,)),
            dma((8,)),
            dma((8,)),
            pltpu.SemaphoreType.REGULAR((ROUNDS,)),
        ],
        compiler_params=pltpu.CompilerParams(
            collective_id=0, has_side_effects=True, vmem_limit_bytes=63_400_000
        ),
        cost_estimate=pl.CostEstimate(
            flops=2 * rows * height * 8 * width, bytes_accessed=6 * 1024 * 1024, transcendentals=0
        ),
    )(
        ancestor_inverse,
        factor_cols,
        diag_inverse,
        pole_weights,
        block_pattern.T,
        supernode_ids.reshape(-1, width),
    )
    out, density = pl.pallas_call(
        hand_over,
        out_shape=(
            jax.ShapeDtypeStruct((rows, 8, width), BF16),
            jax.ShapeDtypeStruct((1, width), F32),
        ),
        in_specs=[vmem, vmem],
        out_specs=(anywhere, anywhere),
        scratch_shapes=[dma((5,))],
        compiler_params=pltpu.CompilerParams(vmem_limit_bytes=16 * 1024 * 1024),
    )(out, density)
    return out.reshape(1, rows, 8, 1, width), density.reshape(width)


def solution(mesh):
    in_specs = (
        P("pole", "row", "col"),
        P("pole", None, ("row", "col")),
        P("pole", ("row", "col")),
        P("pole"),
        P(),
        P(),
    )
    out_specs = (P("pole", "row", None, "col", None), P(("row", "col")))
    return jax.shard_map(per_device, mesh=mesh, in_specs=in_specs, out_specs=out_specs, check_vma=False)
```

```python
import functools

import jax
import jax.numpy as jnp
from jax import lax
from jax.experimental import pallas as pl
from jax.experimental.pallas import tpu as pltpu
from jax.sharding import PartitionSpec as P

MESH = pl.DeviceIdType.MESH
F32, BF16 = jnp.float32, jnp.bfloat16

UNITS = 24
OWN, ZP, YN, YP = (0, 0), (0, 1), (1, 0), (3, 0)
YNZ, YPZ, YF, YFZ = (1, 1), (3, 1), (2, 0), (2, 1)
SLOTS = [OWN, ZP, YN, YP, YNZ, YPZ, YF, YFZ]
NEAR = [YP, YN, ZP]

Y_UP = [
    (OWN, YP, 0, 6), (OWN, YP, 18, 6), (OWN, YP, 12, 6), (OWN, YP, 6, 2),
    (YP, YF, 0, 6), (YP, YF, 18, 6),
    (ZP, YPZ, 0, 6), (ZP, YPZ, 6, 6), (ZP, YPZ, 12, 2),
    (YPZ, YFZ, 0, 3), (YPZ, YFZ, 3, 3),
    (OWN, YP, 8, 3), (OWN, YP, 11, 1),
]
Y_DOWN = [
    (OWN, YN, 12, 6), (OWN, YN, 18, 6), (OWN, YN, 6, 6), (OWN, YN, 0, 2),
    (YN, YF, 12, 6), (YN, YF, 6, 6),
    (ZP, YNZ, 6, 6), (ZP, YNZ, 0, 6), (ZP, YNZ, 12, 2),
    (YNZ, YFZ, 6, 3), (YNZ, YFZ, 9, 3),
    (OWN, YN, 2, 3), (OWN, YN, 5, 1),
]
Z_SWAP = [
    (OWN, ZP, 0, 6), (OWN, ZP, 6, 6), (OWN, ZP, 12, 8),
    (YN, YNZ, 14, 10), (YP, YPZ, 14, 10),
    (YF, YFZ, 12, 6), (YF, YFZ, 18, 3), (YF, YFZ, 21, 3),
    (OWN, ZP, 20, 3), (OWN, ZP, 23, 1),
]
HALVES = [[(0, 10), (20, 10), (40, 4)], [(10, 10), (30, 10), (44, 4)]]
X_UP = [(0, 3, *m) for m in HALVES[0] + HALVES[1]] + [(3, 2, *m) for m in HALVES[0]]
X_DOWN = [(0, 1, *m) for m in HALVES[1] + HALVES[0]] + [(1, 2, *m) for m in HALVES[1]]
CHUNKS = [(0, 20), (20, 40), (40, 48)]
ROUNDS = 4


def at_slot(slot):
    return SLOTS.index(slot)


def kernel(
    a_hbm, f_hbm, diag_hbm, weight_ref, pattern_hbm, ids_hbm,
    out_ref, density_ref,
    a_all, f_all, acc, coarse, wide, diag_ref, pattern_ref, ids_ref, part, red, near, late, pol,
    load_sem, f_send, f_recv, a_send, a_recv, red_send, red_recv, end_send, end_recv, token,
):
    pole, row, col = lax.axis_index("pole"), lax.axis_index("row"), lax.axis_index("col")
    n_pole = lax.axis_size("pole")
    y, z = row // 2, row % 2
    rows, depth = a_all.shape[1], a_all.shape[2]
    unit, part_rows = f_all.shape[1] // UNITS, rows // 48
    blocks = coarse.shape[0] // 4
    rblk = depth // blocks

    def row_of(slot):
        return ((y + slot[0]) % 4) * 2 + (z + slot[1]) % 2

    x_up, x_down = {"col": (col + 1) % 4}, {"col": (col + 3) % 4}
    y_up, y_down, z_swap = {"row": row_of(YN)}, {"row": row_of(YP)}, {"row": row_of(ZP)}
    z_far = {"pole": (pole + n_pole - 2 + 4 * z) % n_pole, "row": row_of(ZP)}
    core = {"pole": pole + 1 - 2 * (pole % 2)}

    def signal(sem, devices):
        for device in devices:
            pl.semaphore_signal(sem, inc=1, device_id=device, device_id_type=MESH)

    own_rows = pltpu.make_async_copy(a_hbm.at[0], a_all.at[0], load_sem.at[4])
    loads = []
    for q in range(4):
        source = pl.ds(pl.multiple_of(((col + q) % 4) * depth, depth), depth)
        loads.append(
            pltpu.make_async_copy(f_hbm.at[0, source], f_all.at[0, pl.ds(q * depth, depth)], load_sem.at[q])
        )
    small = [
        pltpu.make_async_copy(source, target, load_sem.at[5 + i])
        for i, (source, target) in enumerate([(ids_hbm, ids_ref), (pattern_hbm, pattern_ref), (diag_hbm, diag_ref)])
    ]

    barrier = pltpu.get_barrier_semaphore()
    friends = [x_up, x_down, y_up, y_down, z_swap, z_far, core]
    signal(barrier, friends)
    for copy in small:
        copy.start()
    for q in (0, 2, 1, 3):
        loads[q].start()
    own_rows.start()

    def f_copies(link, plan, device):
        copies = []
        for i, (here, there, first, count) in enumerate(plan):
            span = pl.ds(first * unit, count * unit)
            copies.append(
                pltpu.make_async_remote_copy(
                    src_ref=f_all.at[at_slot(here), span],
                    dst_ref=f_all.at[at_slot(there), span],
                    send_sem=f_send.at[link, i],
                    recv_sem=f_recv.at[link, i],
                    device_id=device,
                    device_id_type=MESH,
                )
            )
        return copies

    def a_copies(link, plan, device):
        copies = []
        for i, (here, there, first, count) in enumerate(plan):
            span = pl.ds(first * part_rows, count * part_rows)
            copies.append(
                pltpu.make_async_remote_copy(
                    src_ref=a_hbm.at[0, span] if here == 0 else a_all.at[here, span],
                    dst_ref=a_all.at[there, span],
                    send_sem=a_send.at[link, i],
                    recv_sem=a_recv.at[link, i],
                    device_id=device,
                    device_id_type=MESH,
                )
            )
        return copies

    yu, yd, zs = f_copies(0, Y_UP, y_up), f_copies(1, Y_DOWN, y_down), f_copies(2, Z_SWAP, z_swap)
    xu, xd = a_copies(0, X_UP, x_up), a_copies(1, X_DOWN, x_down)

    def start(copies, *which):
        for i in which:
            copies[i].start()

    def arrived(copies, *which):
        for i in which:
            copies[i].wait_recv()

    for copy in small:
        copy.wait()
    ids = ids_ref[pl.ds(row * 4 + col, 1), :]
    onehot = jnp.where(ids == lax.broadcasted_iota(jnp.int32, (pattern_ref.shape[0], ids.shape[1]), 0), 1.0, 0.0)
    coarse[...] = lax.dot_general(
        pattern_ref[...].astype(F32).astype(BF16), onehot.astype(BF16), (((0,), (0,)), ((), ())),
        preferred_element_type=F32,
    )

    def mask_quarter(q):
        loads[q].wait()
        first = ((col + q) % 4) * blocks

        def body(j, carry):
            span = pl.ds(pl.multiple_of(q * depth + j * rblk, rblk), rblk)
            mask = coarse[pl.ds(first + j, 1), :].astype(BF16)
            f_all[0, span, :] = f_all[0, span, :] * mask
            return carry

        lax.fori_loop(0, blocks, body, 0)

    mask_quarter(0)
    pl.semaphore_wait(barrier, len(friends))
    start(yu, 0)
    start(zs, 0)
    start(xu, 0)
    start(xd, 0)
    mask_quarter(2)
    start(yd, 0)
    mask_quarter(1)
    start(zs, 1)
    mask_quarter(3)
    start(yu, 1)
    start(yd, 1)
    start(yd, 2)
    start(xu, 1)
    start(xd, 1)
    start(yu, 2)
    start(zs, 2)
    start(yu, 3)
    start(yd, 3)
    start(xu, 2, 3, 4, 5)
    start(xd, 2, 3, 4, 5)

    def tokens(which):
        signal(token.at[which], [z_swap, z_far, core])
        pl.semaphore_wait(token.at[which], 3)

    begun = set()

    def product_of(slots, first, count, where):
        q = first * unit // depth
        span = slice(first * unit, (first + count) * unit)
        right = [f_all[at_slot(s), span, :] for s in slots]
        right = right[0] if len(right) == 1 else jnp.concatenate(right, axis=1)
        left = a_all[q, where, first * unit - q * depth : (first + count) * unit - q * depth]
        return jnp.dot(left, right, preferred_element_type=F32)

    def multiply(slots, first, count, chunks=(0, 1, 2)):
        base = CHUNKS[chunks[0]][0] * part_rows
        product = product_of(slots, first, count, slice(base, CHUNKS[chunks[-1]][1] * part_rows))
        width = product.shape[1] // len(slots)
        for i, slot in enumerate(slots):
            for c in chunks:
                s, begin, end = at_slot(slot), CHUNKS[c][0] * part_rows, CHUNKS[c][1] * part_rows
                term = product[begin - base : end - base, i * width : (i + 1) * width]
                acc[s, begin:end, :] = acc[s, begin:end, :] + term if (slot, c) in begun else term
                begun.add((slot, c))

    own_span = pl.ds(pl.multiple_of(((row * rows // depth - col + 4) % 4) * depth + (row * rows) % depth, rows), rows)
    reds = []
    far_first = sorted(range(n_pole), key=lambda d: abs(d - n_pole // 2))

    def place(slot, total):
        wide[pl.ds(row_of(slot), rows, stride=8), :] = total

    def finish(pieces):
        totals = [acc[at_slot(slot)] + product_of([slot], first, count, slice(0, rows)) for slot, first, count in pieces]
        for (slot, _, _), total in zip(pieces, totals):
            k, back = NEAR.index(slot), NEAR.index(((-slot[0]) % 4, slot[1]))
            near[k] = weight_ref[0] * jnp.sum(row_sums(slot, total), axis=0, keepdims=True)
            for d in far_first:
                pltpu.make_async_remote_copy(
                    src_ref=near.at[k],
                    dst_ref=late.at[back, pole],
                    send_sem=end_send.at[0],
                    recv_sem=end_recv.at[0],
                    device_id={"pole": (pole + d) % n_pole, "row": row_of(slot)},
                    device_id_type=MESH,
                ).start()
        for (slot, _, _), total in zip(pieces, totals):
            place(slot, total)

    def row_sums(slot, total):
        terms = f_all[at_slot(slot), own_span, :].astype(F32) * total
        return jnp.sum(terms.reshape(rows // 8, 8, terms.shape[1]), axis=0)

    def reduce_rows(slot, total):
        s = at_slot(slot)
        sums = row_sums(slot, total)
        if slot == OWN:
            red[0] = sums
            return
        part[s] = sums
        back = at_slot(((-slot[0]) % 4, slot[1]))
        copy = pltpu.make_async_remote_copy(
            src_ref=part.at[s],
            dst_ref=red.at[back],
            send_sem=red_send.at[s],
            recv_sem=red_recv.at[back],
            device_id={"row": row_of(slot)},
            device_id_type=MESH,
        )
        copy.start()
        reds.append(copy)

    own_rows.wait()
    arrived(zs, 0)
    multiply([OWN, ZP], 0, 6)
    arrived(yu, 0, 1)
    start(yu, 4, 5)
    arrived(yd, 0, 1)
    start(zs, 3)
    start(yd, 4)
    tokens(0)
    arrived(yd, 2)
    start(yd, 5)
    arrived(xu, 0, 1, 2)
    start(xu, 6, 7, 8)
    arrived(xd, 0, 1, 2)
    start(xd, 6, 7, 8)
    arrived(zs, 1, 2)
    start(yu, 6, 7, 8)
    start(yd, 6, 7, 8)
    arrived(yu, 2)
    start(zs, 4)
    tokens(1)
    arrived(yu, 3)
    arrived(yd, 3)
    multiply([YN, YP], 0, 2)
    multiply([YP], 2, 4)
    tokens(2)
    arrived(yu, 4, 5)
    arrived(yd, 4, 5)
    start(zs, 5, 6, 7, 8, 9)
    tokens(3)
    arrived(xu, 3, 4, 5)
    arrived(xd, 3, 4, 5)
    multiply([OWN, ZP], 6, 6)
    multiply([OWN, ZP], 18, 2)
    multiply([OWN], 20, 4)
    arrived(yu, 6)
    start(yu, 9, 10, 11, 12)
    arrived(yd, 6)
    start(yd, 9, 10, 11, 12)
    multiply([YN, YP], 6, 2)
    multiply([YN], 8, 4)
    multiply([YN, YP], 18, 6)
    arrived(zs, 3, 4)
    multiply([YNZ, YPZ], 18, 6)
    arrived(yu, 7)
    arrived(yd, 7)
    multiply([YNZ, YPZ], 0, 6)
    multiply([YNZ, YPZ], 6, 6)
    arrived(xu, 6)
    arrived(xd, 6)
    arrived(yu, 8)
    arrived(yd, 8)
    arrived(zs, 5)
    multiply(SLOTS, 12, 6, (0,))
    arrived(yu, 9)
    arrived(yd, 9)
    arrived(zs, 6)
    multiply([YF, YFZ], 0, 3)
    multiply([YF, YFZ], 6, 3)
    multiply([YF, YFZ], 18, 3)
    arrived(xu, 7)
    arrived(xd, 7)
    multiply(SLOTS, 12, 6, (1,))
    arrived(yu, 10)
    arrived(yd, 10)
    arrived(zs, 7)
    multiply([YF, YFZ], 3, 3)
    multiply([YF, YFZ], 9, 3)
    multiply([YF, YFZ], 21, 3)
    arrived(xu, 8)
    arrived(xd, 8)
    multiply(SLOTS, 12, 6, (2,))
    for slot in (YFZ, YF, YNZ, YPZ, OWN):
        reduce_rows(slot, acc[at_slot(slot)])
    arrived(yu, 11)
    arrived(yd, 11)
    arrived(zs, 8)
    multiply([YP], 8, 3)
    multiply([YN], 2, 3)
    multiply([ZP], 20, 3)
    arrived(yu, 12)
    arrived(yd, 12)
    arrived(zs, 9)
    finish([(YP, 11, 1), (YN, 5, 1), (ZP, 23, 1)])

    for copy in reds:
        copy.wait_recv()
    total = red[at_slot(OWN)]
    for slot in (YNZ, YPZ, YF, YFZ):
        total = total + red[at_slot(slot)]
    pol[pole] = weight_ref[0] * (diag_ref[...] + jnp.sum(total, axis=0, keepdims=True))
    for d in far_first:
        if d > 0:
            pltpu.make_async_remote_copy(
                src_ref=pol.at[pole],
                dst_ref=pol.at[pole],
                send_sem=end_send.at[1],
                recv_sem=end_recv.at[1],
                device_id={"pole": (pole + d) % n_pole},
                device_id_type=MESH,
            ).start()

    for slot in (OWN, YNZ, YPZ, YF, YFZ):
        place(slot, acc[at_slot(slot)])

    def body(j, carry):
        base = pl.multiple_of(j * 32, 32)
        block = wide[pl.ds(pl.multiple_of(base * 8, 256), 256), :]
        out_ref[pl.ds(base, 32)] = (-block).reshape(32, 8, block.shape[1]).astype(BF16)
        return carry

    lax.fori_loop(0, rows // 32, body, 0)

    for copies in (yu, yd, zs, xu, xd, reds):
        for copy in copies:
            copy.wait_send()
    for i, whole in enumerate((late, pol.at[pl.ds(0, n_pole - 1)])):
        every = pltpu.make_async_remote_copy(
            src_ref=whole,
            dst_ref=whole,
            send_sem=end_send.at[i],
            recv_sem=end_recv.at[i],
            device_id=core,
            device_id_type=MESH,
        )
        every.wait()
    density = jnp.zeros(density_ref.shape, F32)
    for p in range(n_pole):
        density = density + ((pol[p] + late[0, p]) + (late[1, p] + late[2, p]))
    density_ref[...] = density


def hand_over(out_ref, density_ref, out_hbm, density_hbm, sems):
    rows = out_ref.shape[0]
    copies = [pltpu.make_async_copy(density_ref, density_hbm, sems.at[4])]
    for i in range(4):
        span = pl.ds(i * (rows // 4), rows // 4)
        copies.append(pltpu.make_async_copy(out_ref.at[span], out_hbm.at[span], sems.at[i]))
    for copy in copies:
        copy.start()
    for copy in copies:
        copy.wait()


def per_device(ancestor_inverse, factor_cols, diag_inverse, pole_weights, block_pattern, supernode_ids):
    _, rows, depth = ancestor_inverse.shape
    _, height, width = factor_cols.shape
    blocks = block_pattern.shape[0]
    vmem = pl.BlockSpec(memory_space=pltpu.VMEM)
    anywhere = pl.BlockSpec(memory_space=pl.ANY)
    dma = pltpu.SemaphoreType.DMA
    links = max(len(Y_UP), len(Z_SWAP))
    out, density = pl.pallas_call(
        kernel,
        out_shape=(
            pltpu.VMEM((rows, 8, width), BF16),
            pltpu.VMEM((1, width), F32),
        ),
        in_specs=[anywhere, anywhere, anywhere, pl.BlockSpec(memory_space=pltpu.SMEM), anywhere, anywhere],
        out_specs=(vmem, vmem),
        scratch_shapes=[
            pltpu.VMEM((4, rows, depth), BF16),
            pltpu.VMEM((8, height, width), BF16),
            pltpu.VMEM((8, rows, width), F32),
            pltpu.VMEM((blocks, width), F32),
            pltpu.VMEM((rows * 8, width), F32),
            pltpu.VMEM((1, width), F32),
            pltpu.VMEM(block_pattern.shape[::-1], jnp.int32),
            pltpu.VMEM((supernode_ids.size // width, width), jnp.int32),
            pltpu.VMEM((8, 8, width), F32),
            pltpu.VMEM((8, 8, width), F32),
            pltpu.VMEM((len(NEAR), 1, width), F32),
            pltpu.VMEM((len(NEAR), 8, 1, width), F32),
            pltpu.VMEM((8, 1, width), F32),
            dma((8,)),
            dma((3, links)),
            dma((3, links)),
            dma((2, len(X_UP))),
            dma((2, len(X_UP))),
            dma((8,)),
            dma((8,)),
            dma((2,)),
            dma((2,)),
            pltpu.SemaphoreType.REGULAR((ROUNDS,)),
        ],
        compiler_params=pltpu.CompilerParams(
            collective_id=0, has_side_effects=True, vmem_limit_bytes=63_400_000
        ),
        cost_estimate=pl.CostEstimate(
            flops=2 * rows * height * 8 * width, bytes_accessed=6 * 1024 * 1024, transcendentals=0
        ),
    )(
        ancestor_inverse,
        factor_cols,
        diag_inverse,
        pole_weights,
        block_pattern.T,
        supernode_ids.reshape(-1, width),
    )
    out, density = pl.pallas_call(
        hand_over,
        out_shape=(
            jax.ShapeDtypeStruct((rows, 8, width), BF16),
            jax.ShapeDtypeStruct((1, width), F32),
        ),
        in_specs=[vmem, vmem],
        out_specs=(anywhere, anywhere),
        scratch_shapes=[dma((5,))],
        compiler_params=pltpu.CompilerParams(vmem_limit_bytes=16 * 1024 * 1024),
    )(out, density)
    return out.reshape(1, rows, 8, 1, width), density.reshape(width)


def solution(mesh):
    in_specs = (
        P("pole", "row", "col"),
        P("pole", None, ("row", "col")),
        P("pole", ("row", "col")),
        P("pole"),
        P(),
        P(),
    )
    out_specs = (P("pole", "row", None, "col", None), P(("row", "col")))
    return jax.shard_map(per_device, mesh=mesh, in_specs=in_specs, out_specs=out_specs, check_vma=False)
```

```python
import functools

import jax
import jax.numpy as jnp
from jax import lax
from jax.experimental import pallas as pl
from jax.experimental.pallas import tpu as pltpu
from jax.sharding import PartitionSpec as P

MESH = pl.DeviceIdType.MESH
F32, BF16 = jnp.float32, jnp.bfloat16

UNITS = 24
OWN, ZP, YN, YP = (0, 0), (0, 1), (1, 0), (3, 0)
YNZ, YPZ, YF, YFZ = (1, 1), (3, 1), (2, 0), (2, 1)
SLOTS = [OWN, ZP, YN, YP, YNZ, YPZ, YF, YFZ]
NEAR = [YP, YN, ZP]

Y_UP = [
    (OWN, YP, 0, 6), (OWN, YP, 18, 6), (OWN, YP, 12, 6), (OWN, YP, 6, 2),
    (YP, YF, 0, 6), (YP, YF, 18, 6),
    (ZP, YPZ, 0, 6), (ZP, YPZ, 6, 6), (ZP, YPZ, 12, 2),
    (YPZ, YFZ, 0, 3), (YPZ, YFZ, 3, 3),
    (OWN, YP, 8, 3), (OWN, YP, 11, 1),
]
Y_DOWN = [
    (OWN, YN, 12, 6), (OWN, YN, 18, 6), (OWN, YN, 6, 6), (OWN, YN, 0, 2),
    (YN, YF, 12, 6), (YN, YF, 6, 6),
    (ZP, YNZ, 6, 6), (ZP, YNZ, 0, 6), (ZP, YNZ, 12, 2),
    (YNZ, YFZ, 6, 3), (YNZ, YFZ, 9, 3),
    (OWN, YN, 2, 3), (OWN, YN, 5, 1),
]
Z_SWAP = [
    (OWN, ZP, 0, 6), (OWN, ZP, 6, 6), (OWN, ZP, 12, 8),
    (YN, YNZ, 14, 10), (YP, YPZ, 14, 10),
    (YF, YFZ, 12, 6), (YF, YFZ, 18, 3), (YF, YFZ, 21, 3),
    (OWN, ZP, 20, 3), (OWN, ZP, 23, 1),
]
HALVES = [[(0, 10), (20, 10), (40, 4)], [(10, 10), (30, 10), (44, 4)]]
X_UP = [(0, 3, *m) for m in HALVES[0] + HALVES[1]] + [(3, 2, *m) for m in HALVES[0]]
X_DOWN = [(0, 1, *m) for m in HALVES[1] + HALVES[0]] + [(1, 2, *m) for m in HALVES[1]]
CHUNKS = [(0, 20), (20, 40), (40, 48)]
ROUNDS = 4


def at_slot(slot):
    return SLOTS.index(slot)


def kernel(
    a_hbm, f_hbm, diag_hbm, weight_ref, pattern_hbm, ids_hbm,
    out_ref, density_ref,
    a_all, f_all, acc, coarse, wide, diag_ref, pattern_ref, ids_ref, part, red, near, late, pol,
    load_sem, f_send, f_recv, a_send, a_recv, red_send, red_recv, end_send, end_recv, token,
):
    pole, row, col = lax.axis_index("pole"), lax.axis_index("row"), lax.axis_index("col")
    n_pole = lax.axis_size("pole")
    y, z = row // 2, row % 2
    rows, depth = a_all.shape[1], a_all.shape[2]
    unit, part_rows = f_all.shape[1] // UNITS, rows // 48
    blocks = coarse.shape[0] // 4
    rblk = depth // blocks

    def row_of(slot):
        return ((y + slot[0]) % 4) * 2 + (z + slot[1]) % 2

    x_up, x_down = {"col": (col + 1) % 4}, {"col": (col + 3) % 4}
    y_up, y_down, z_swap = {"row": row_of(YN)}, {"row": row_of(YP)}, {"row": row_of(ZP)}
    z_far = {"pole": (pole + n_pole - 2 + 4 * z) % n_pole, "row": row_of(ZP)}
    core = {"pole": pole + 1 - 2 * (pole % 2)}

    def signal(sem, devices):
        for device in devices:
            pl.semaphore_signal(sem, inc=1, device_id=device, device_id_type=MESH)

    own_rows = pltpu.make_async_copy(a_hbm.at[0], a_all.at[0], load_sem.at[4])
    loads = []
    for q in range(4):
        source = pl.ds(pl.multiple_of(((col + q) % 4) * depth, depth), depth)
        loads.append(
            pltpu.make_async_copy(f_hbm.at[0, source], f_all.at[0, pl.ds(q * depth, depth)], load_sem.at[q])
        )
    small = [
        pltpu.make_async_copy(source, target, load_sem.at[5 + i])
        for i, (source, target) in enumerate([(ids_hbm, ids_ref), (pattern_hbm, pattern_ref), (diag_hbm, diag_ref)])
    ]

    barrier = pltpu.get_barrier_semaphore()
    friends = [x_up, x_down, y_up, y_down, z_swap, z_far, core]
    signal(barrier, friends)
    for copy in small:
        copy.start()
    for q in (0, 2, 1, 3):
        loads[q].start()
    own_rows.start()

    def f_copies(link, plan, device):
        copies = []
        for i, (here, there, first, count) in enumerate(plan):
            span = pl.ds(first * unit, count * unit)
            copies.append(
                pltpu.make_async_remote_copy(
                    src_ref=f_all.at[at_slot(here), span],
                    dst_ref=f_all.at[at_slot(there), span],
                    send_sem=f_send.at[link, i],
                    recv_sem=f_recv.at[link, i],
                    device_id=device,
                    device_id_type=MESH,
                )
            )
        return copies

    def a_copies(link, plan, device):
        copies = []
        for i, (here, there, first, count) in enumerate(plan):
            span = pl.ds(first * part_rows, count * part_rows)
            copies.append(
                pltpu.make_async_remote_copy(
                    src_ref=a_hbm.at[0, span] if here == 0 else a_all.at[here, span],
                    dst_ref=a_all.at[there, span],
                    send_sem=a_send.at[link, i],
                    recv_sem=a_recv.at[link, i],
                    device_id=device,
                    device_id_type=MESH,
                )
            )
        return copies

    yu, yd, zs = f_copies(0, Y_UP, y_up), f_copies(1, Y_DOWN, y_down), f_copies(2, Z_SWAP, z_swap)
    xu, xd = a_copies(0, X_UP, x_up), a_copies(1, X_DOWN, x_down)

    def start(copies, *which):
        for i in which:
            copies[i].start()

    def arrived(copies, *which):
        for i in which:
            copies[i].wait_recv()

    for copy in small:
        copy.wait()
    ids = ids_ref[pl.ds(row * 4 + col, 1), :]
    onehot = jnp.where(ids == lax.broadcasted_iota(jnp.int32, (pattern_ref.shape[0], ids.shape[1]), 0), 1.0, 0.0)
    coarse[...] = lax.dot_general(
        pattern_ref[...].astype(F32).astype(BF16), onehot.astype(BF16), (((0,), (0,)), ((), ())),
        preferred_element_type=F32,
    )

    def mask_quarter(q):
        loads[q].wait()
        first = ((col + q) % 4) * blocks

        def body(j, carry):
            span = pl.ds(pl.multiple_of(q * depth + j * rblk, rblk), rblk)
            mask = coarse[pl.ds(first + j, 1), :].astype(BF16)
            f_all[0, span, :] = f_all[0, span, :] * mask
            return carry

        lax.fori_loop(0, blocks, body, 0)

    mask_quarter(0)
    pl.semaphore_wait(barrier, len(friends))
    start(yu, 0)
    start(zs, 0)
    start(xu, 0)
    start(xd, 0)
    mask_quarter(2)
    start(yd, 0)
    mask_quarter(1)
    start(zs, 1)
    mask_quarter(3)
    start(yu, 1)
    start(yd, 1)
    start(yd, 2)
    start(xu, 1)
    start(xd, 1)
    start(yu, 2)
    start(zs, 2)
    start(yu, 3)
    start(yd, 3)
    start(xu, 2, 3, 4, 5)
    start(xd, 2, 3, 4, 5)

    def tokens(which):
        signal(token.at[which], [z_swap, z_far, core])
        pl.semaphore_wait(token.at[which], 3)

    begun = set()

    def product_of(slots, first, count, where):
        q = first * unit // depth
        span = slice(first * unit, (first + count) * unit)
        right = [f_all[at_slot(s), span, :] for s in slots]
        right = right[0] if len(right) == 1 else jnp.concatenate(right, axis=1)
        left = a_all[q, where, first * unit - q * depth : (first + count) * unit - q * depth]
        return jnp.dot(left, right, preferred_element_type=F32)

    def multiply(slots, first, count, chunks=(0, 1, 2)):
        base = CHUNKS[chunks[0]][0] * part_rows
        product = product_of(slots, first, count, slice(base, CHUNKS[chunks[-1]][1] * part_rows))
        width = product.shape[1] // len(slots)
        for i, slot in enumerate(slots):
            for c in chunks:
                s, begin, end = at_slot(slot), CHUNKS[c][0] * part_rows, CHUNKS[c][1] * part_rows
                term = product[begin - base : end - base, i * width : (i + 1) * width]
                acc[s, begin:end, :] = acc[s, begin:end, :] + term if (slot, c) in begun else term
                begun.add((slot, c))

    own_span = pl.ds(pl.multiple_of(((row * rows // depth - col + 4) % 4) * depth + (row * rows) % depth, rows), rows)
    reds = []
    far_first = sorted(range(n_pole), key=lambda d: abs(d - n_pole // 2))

    def place(slot, total):
        wide[pl.ds(row_of(slot), rows, stride=8), :] = total

    def finish(pieces):
        totals = [acc[at_slot(slot)] + product_of([slot], first, count, slice(0, rows)) for slot, first, count in pieces]
        for (slot, _, _), total in zip(pieces, totals):
            k, back = NEAR.index(slot), NEAR.index(((-slot[0]) % 4, slot[1]))
            near[k] = weight_ref[0] * jnp.sum(row_sums(slot, total), axis=0, keepdims=True)
            for d in far_first:
                pltpu.make_async_remote_copy(
                    src_ref=near.at[k],
                    dst_ref=late.at[back, pole],
                    send_sem=end_send.at[0],
                    recv_sem=end_recv.at[0],
                    device_id={"pole": (pole + d) % n_pole, "row": row_of(slot)},
                    device_id_type=MESH,
                ).start()
        for (slot, _, _), total in zip(pieces, totals):
            place(slot, total)

    def row_sums(slot, total):
        terms = f_all[at_slot(slot), own_span, :].astype(F32) * total
        return jnp.sum(terms.reshape(rows // 8, 8, terms.shape[1]), axis=0)

    def reduce_rows(slot, total):
        s = at_slot(slot)
        sums = row_sums(slot, total)
        if slot == OWN:
            red[0] = sums
            return
        part[s] = sums
        back = at_slot(((-slot[0]) % 4, slot[1]))
        copy = pltpu.make_async_remote_copy(
            src_ref=part.at[s],
            dst_ref=red.at[back],
            send_sem=red_send.at[s],
            recv_sem=red_recv.at[back],
            device_id={"row": row_of(slot)},
            device_id_type=MESH,
        )
        copy.start()
        reds.append(copy)

    own_rows.wait()
    arrived(zs, 0)
    multiply([OWN, ZP], 0, 6)
    arrived(yu, 0, 1)
    start(yu, 4, 5)
    arrived(yd, 0, 1)
    start(zs, 3)
    start(yd, 4)
    tokens(0)
    arrived(yd, 2)
    start(yd, 5)
    arrived(xu, 0, 1, 2)
    start(xu, 6, 7, 8)
    arrived(xd, 0, 1, 2)
    start(xd, 6, 7, 8)
    arrived(zs, 1, 2)
    start(yu, 6, 7, 8)
    start(yd, 6, 7, 8)
    arrived(yu, 2)
    start(zs, 4)
    tokens(1)
    arrived(yu, 3)
    arrived(yd, 3)
    multiply([YN, YP], 0, 2)
    multiply([YP], 2, 4)
    tokens(2)
    arrived(yu, 4, 5)
    arrived(yd, 4, 5)
    start(zs, 5, 6, 7, 8, 9)
    tokens(3)
    arrived(xu, 3, 4, 5)
    arrived(xd, 3, 4, 5)
    multiply([OWN, ZP], 6, 6)
    multiply([OWN, ZP], 18, 2)
    multiply([OWN], 20, 4)
    arrived(yu, 6)
    start(yu, 9, 10, 11, 12)
    arrived(yd, 6)
    start(yd, 9, 10, 11, 12)
    multiply([YN, YP], 6, 2)
    multiply([YN], 8, 4)
    multiply([YN, YP], 18, 6)
    arrived(zs, 3, 4)
    multiply([YNZ, YPZ], 18, 6)
    arrived(yu, 7)
    arrived(yd, 7)
    multiply([YNZ, YPZ], 0, 6)
    multiply([YNZ, YPZ], 6, 6)
    arrived(xu, 6)
    arrived(xd, 6)
    arrived(yu, 8)
    arrived(yd, 8)
    arrived(zs, 5)
    multiply(SLOTS, 12, 6, (0,))
    arrived(yu, 9)
    arrived(yd, 9)
    arrived(zs, 6)
    multiply([YF, YFZ], 0, 3)
    multiply([YF, YFZ], 6, 3)
    multiply([YF, YFZ], 18, 3)
    arrived(xu, 7)
    arrived(xd, 7)
    multiply(SLOTS, 12, 6, (1,))
    arrived(yu, 10)
    arrived(yd, 10)
    arrived(zs, 7)
    multiply([YF, YFZ], 3, 3)
    multiply([YF, YFZ], 9, 3)
    multiply([YF, YFZ], 21, 3)
    arrived(xu, 8)
    arrived(xd, 8)
    multiply(SLOTS, 12, 6, (2,))
    for slot in (YFZ, YF, YNZ, YPZ, OWN):
        reduce_rows(slot, acc[at_slot(slot)])
    arrived(yu, 11)
    arrived(yd, 11)
    arrived(zs, 8)
    multiply([YP], 8, 3)
    multiply([YN], 2, 3)
    multiply([ZP], 20, 3)
    arrived(yu, 12)
    arrived(yd, 12)
    arrived(zs, 9)
    finish([(YP, 11, 1), (YN, 5, 1), (ZP, 23, 1)])

    for copy in reds:
        copy.wait_recv()
    total = red[at_slot(OWN)]
    for slot in (YNZ, YPZ, YF, YFZ):
        total = total + red[at_slot(slot)]
    pol[pole] = weight_ref[0] * (diag_ref[...] + jnp.sum(total, axis=0, keepdims=True))
    for d in far_first:
        if d > 0:
            pltpu.make_async_remote_copy(
                src_ref=pol.at[pole],
                dst_ref=pol.at[pole],
                send_sem=end_send.at[1],
                recv_sem=end_recv.at[1],
                device_id={"pole": (pole + d) % n_pole},
                device_id_type=MESH,
            ).start()

    for slot in (OWN, YNZ, YPZ, YF, YFZ):
        place(slot, acc[at_slot(slot)])

    def body(j, carry):
        base = pl.multiple_of(j * 32, 32)
        block = wide[pl.ds(pl.multiple_of(base * 8, 256), 256), :]
        out_ref[pl.ds(base, 32)] = (-block).reshape(32, 8, block.shape[1]).astype(BF16)
        return carry

    lax.fori_loop(0, rows // 32, body, 0)

    for copies in (yu, yd, zs, xu, xd, reds):
        for copy in copies:
            copy.wait_send()
    for i, whole in enumerate((late, pol.at[pl.ds(0, n_pole - 1)])):
        every = pltpu.make_async_remote_copy(
            src_ref=whole,
            dst_ref=whole,
            send_sem=end_send.at[i],
            recv_sem=end_recv.at[i],
            device_id=core,
            device_id_type=MESH,
        )
        every.wait()
    density = jnp.zeros(density_ref.shape, F32)
    for p in range(n_pole):
        density = density + ((pol[p] + late[0, p]) + (late[1, p] + late[2, p]))
    density_ref[...] = density


def hand_over(out_ref, density_ref, out_hbm, density_hbm, sems):
    rows = out_ref.shape[0]
    copies = [pltpu.make_async_copy(density_ref, density_hbm, sems.at[4])]
    for i in range(4):
        span = pl.ds(i * (rows // 4), rows // 4)
        copies.append(pltpu.make_async_copy(out_ref.at[span], out_hbm.at[span], sems.at[i]))
    for copy in copies:
        copy.start()
    for copy in copies:
        copy.wait()


def per_device(ancestor_inverse, factor_cols, diag_inverse, pole_weights, block_pattern, supernode_ids):
    _, rows, depth = ancestor_inverse.shape
    _, height, width = factor_cols.shape
    blocks = block_pattern.shape[0]
    vmem = pl.BlockSpec(memory_space=pltpu.VMEM)
    anywhere = pl.BlockSpec(memory_space=pl.ANY)
    dma = pltpu.SemaphoreType.DMA
    links = max(len(Y_UP), len(Z_SWAP))
    out, density = pl.pallas_call(
        kernel,
        out_shape=(
            pltpu.VMEM((rows, 8, width), BF16),
            pltpu.VMEM((1, width), F32),
        ),
        in_specs=[anywhere, anywhere, anywhere, pl.BlockSpec(memory_space=pltpu.SMEM), anywhere, anywhere],
        out_specs=(vmem, vmem),
        scratch_shapes=[
            pltpu.VMEM((4, rows, depth), BF16),
            pltpu.VMEM((8, height, width), BF16),
            pltpu.VMEM((8, rows, width), F32),
            pltpu.VMEM((blocks, width), F32),
            pltpu.VMEM((rows * 8 + 64, width), F32),
            pltpu.VMEM((1, width), F32),
            pltpu.VMEM(block_pattern.shape[::-1], jnp.int32),
            pltpu.VMEM((supernode_ids.size // width, width), jnp.int32),
            pltpu.VMEM((8, 8, width), F32),
            pltpu.VMEM((8, 8, width), F32),
            pltpu.VMEM((len(NEAR), 1, width), F32),
            pltpu.VMEM((len(NEAR), 8, 1, width), F32),
            pltpu.VMEM((8, 1, width), F32),
            dma((8,)),
            dma((3, links)),
            dma((3, links)),
            dma((2, len(X_UP))),
            dma((2, len(X_UP))),
            dma((8,)),
            dma((8,)),
            dma((2,)),
            dma((2,)),
            pltpu.SemaphoreType.REGULAR((ROUNDS,)),
        ],
        compiler_params=pltpu.CompilerParams(
            collective_id=0, has_side_effects=True, vmem_limit_bytes=63_400_000
        ),
        cost_estimate=pl.CostEstimate(
            flops=2 * rows * height * 8 * width, bytes_accessed=6 * 1024 * 1024, transcendentals=0
        ),
    )(
        ancestor_inverse,
        factor_cols,
        diag_inverse,
        pole_weights,
        block_pattern.T,
        supernode_ids.reshape(-1, width),
    )
    out, density = pl.pallas_call(
        hand_over,
        out_shape=(
            jax.ShapeDtypeStruct((rows, 8, width), BF16),
            jax.ShapeDtypeStruct((1, width), F32),
        ),
        in_specs=[vmem, vmem],
        out_specs=(anywhere, anywhere),
        scratch_shapes=[dma((5,))],
        compiler_params=pltpu.CompilerParams(vmem_limit_bytes=16 * 1024 * 1024),
    )(out, density)
    return out.reshape(1, rows, 8, 1, width), density.reshape(width)


def solution(mesh):
    in_specs = (
        P("pole", "row", "col"),
        P("pole", None, ("row", "col")),
        P("pole", ("row", "col")),
        P("pole"),
        P(),
        P(),
    )
    out_specs = (P("pole", "row", None, "col", None), P(("row", "col")))
    return jax.shard_map(per_device, mesh=mesh, in_specs=in_specs, out_specs=out_specs, check_vma=False)
```

```python
import functools

import jax
import jax.numpy as jnp
from jax import lax
from jax.experimental import pallas as pl
from jax.experimental.pallas import tpu as pltpu
from jax.sharding import PartitionSpec as P

MESH = pl.DeviceIdType.MESH
F32, BF16 = jnp.float32, jnp.bfloat16

UNITS = 24
OWN, ZP, YN, YP = (0, 0), (0, 1), (1, 0), (3, 0)
YNZ, YPZ, YF, YFZ = (1, 1), (3, 1), (2, 0), (2, 1)
SLOTS = [OWN, ZP, YN, YP, YNZ, YPZ, YF, YFZ]
NEAR = [YP, YN, ZP]
FAR = [YFZ, YF, YNZ, YPZ, OWN]

Y_UP = [
    (OWN, YP, 0, 6), (OWN, YP, 18, 6), (OWN, YP, 12, 6), (OWN, YP, 6, 2),
    (YP, YF, 0, 6), (YP, YF, 18, 6),
    (ZP, YPZ, 0, 6), (ZP, YPZ, 6, 6), (ZP, YPZ, 12, 2),
    (YPZ, YFZ, 0, 3), (YPZ, YFZ, 3, 3),
    (OWN, YP, 8, 3), (OWN, YP, 11, 1),
]
Y_DOWN = [
    (OWN, YN, 12, 6), (OWN, YN, 18, 6), (OWN, YN, 6, 6), (OWN, YN, 0, 2),
    (YN, YF, 12, 6), (YN, YF, 6, 6),
    (ZP, YNZ, 6, 6), (ZP, YNZ, 0, 6), (ZP, YNZ, 12, 2),
    (YNZ, YFZ, 6, 3), (YNZ, YFZ, 9, 3),
    (OWN, YN, 2, 3), (OWN, YN, 5, 1),
]
Z_SWAP = [
    (OWN, ZP, 0, 6), (OWN, ZP, 6, 6), (OWN, ZP, 12, 8),
    (YN, YNZ, 14, 10), (YP, YPZ, 14, 10),
    (YF, YFZ, 12, 6), (YF, YFZ, 18, 3), (YF, YFZ, 21, 3),
    (OWN, ZP, 20, 3), (OWN, ZP, 23, 1),
]
HALVES = [[(0, 11), (22, 11), (44, 2)], [(11, 11), (33, 11), (46, 2)]]
X_UP = [(0, 3, *m) for m in HALVES[0] + HALVES[1]] + [(3, 2, *m) for m in HALVES[0]]
X_DOWN = [(0, 1, *m) for m in HALVES[1] + HALVES[0]] + [(1, 2, *m) for m in HALVES[1]]
CHUNKS = [(0, 22), (22, 44), (44, 48)]
ROUNDS = 4


def at_slot(slot):
    return SLOTS.index(slot)


def kernel(
    a_hbm, f_hbm, diag_hbm, weight_ref, pattern_hbm, ids_hbm,
    out_ref, density_ref,
    a_all, f_all, acc, coarse, wide, diag_ref, pattern_ref, ids_ref, part, red, near, late, pol,
    load_sem, f_send, f_recv, a_send, a_recv, red_send, red_recv, end_send, end_recv, token,
):
    pole, row, col = lax.axis_index("pole"), lax.axis_index("row"), lax.axis_index("col")
    n_pole = lax.axis_size("pole")
    y, z = row // 2, row % 2
    rows, depth = a_all.shape[1], a_all.shape[2]
    unit, part_rows = f_all.shape[1] // UNITS, rows // 48
    blocks = coarse.shape[0] // 4
    rblk = depth // blocks

    def row_of(slot):
        return ((y + slot[0]) % 4) * 2 + (z + slot[1]) % 2

    x_up, x_down = {"col": (col + 1) % 4}, {"col": (col + 3) % 4}
    y_up, y_down, z_swap = {"row": row_of(YN)}, {"row": row_of(YP)}, {"row": row_of(ZP)}
    z_far = {"pole": (pole + n_pole - 2 + 4 * z) % n_pole, "row": row_of(ZP)}
    core = {"pole": pole + 1 - 2 * (pole % 2)}

    def signal(sem, devices):
        for device in devices:
            pl.semaphore_signal(sem, inc=1, device_id=device, device_id_type=MESH)

    own_rows = pltpu.make_async_copy(a_hbm.at[0], a_all.at[0], load_sem.at[4])
    loads = []
    for q in range(4):
        source = pl.ds(pl.multiple_of(((col + q) % 4) * depth, depth), depth)
        loads.append(
            pltpu.make_async_copy(f_hbm.at[0, source], f_all.at[0, pl.ds(q * depth, depth)], load_sem.at[q])
        )
    small = [
        pltpu.make_async_copy(source, target, load_sem.at[5 + i])
        for i, (source, target) in enumerate([(ids_hbm, ids_ref), (pattern_hbm, pattern_ref), (diag_hbm, diag_ref)])
    ]

    barrier = pltpu.get_barrier_semaphore()
    friends = [x_up, x_down, y_up, y_down, z_swap, z_far, core]
    signal(barrier, friends)
    for copy in small:
        copy.start()
    for q in (0, 2, 1, 3):
        loads[q].start()
    own_rows.start()

    def f_copies(link, plan, device):
        copies = []
        for i, (here, there, first, count) in enumerate(plan):
            span = pl.ds(first * unit, count * unit)
            copies.append(
                pltpu.make_async_remote_copy(
                    src_ref=f_all.at[at_slot(here), span],
                    dst_ref=f_all.at[at_slot(there), span],
                    send_sem=f_send.at[link, i],
                    recv_sem=f_recv.at[link, i],
                    device_id=device,
                    device_id_type=MESH,
                )
            )
        return copies

    def a_copies(link, plan, device):
        copies = []
        for i, (here, there, first, count) in enumerate(plan):
            span = pl.ds(first * part_rows, count * part_rows)
            copies.append(
                pltpu.make_async_remote_copy(
                    src_ref=a_hbm.at[0, span] if here == 0 else a_all.at[here, span],
                    dst_ref=a_all.at[there, span],
                    send_sem=a_send.at[link, i],
                    recv_sem=a_recv.at[link, i],
                    device_id=device,
                    device_id_type=MESH,
                )
            )
        return copies

    yu, yd, zs = f_copies(0, Y_UP, y_up), f_copies(1, Y_DOWN, y_down), f_copies(2, Z_SWAP, z_swap)
    xu, xd = a_copies(0, X_UP, x_up), a_copies(1, X_DOWN, x_down)

    def start(copies, *which):
        for i in which:
            copies[i].start()

    def arrived(copies, *which):
        for i in which:
            copies[i].wait_recv()

    for copy in small:
        copy.wait()
    ids = ids_ref[pl.ds(row * 4 + col, 1), :]
    onehot = jnp.where(ids == lax.broadcasted_iota(jnp.int32, (pattern_ref.shape[0], ids.shape[1]), 0), 1.0, 0.0)
    coarse[...] = lax.dot_general(
        pattern_ref[...].astype(F32).astype(BF16), onehot.astype(BF16), (((0,), (0,)), ((), ())),
        preferred_element_type=F32,
    )

    def mask_quarter(q):
        loads[q].wait()
        first = ((col + q) % 4) * blocks

        def body(j, carry):
            span = pl.ds(pl.multiple_of(q * depth + j * rblk, rblk), rblk)
            mask = coarse[pl.ds(first + j, 1), :].astype(BF16)
            f_all[0, span, :] = f_all[0, span, :] * mask
            return carry

        lax.fori_loop(0, blocks, body, 0)

    mask_quarter(0)
    pl.semaphore_wait(barrier, len(friends))
    start(yu, 0)
    start(zs, 0)
    start(xu, 0)
    start(xd, 0)
    mask_quarter(2)
    start(yd, 0)
    mask_quarter(1)
    start(zs, 1)
    mask_quarter(3)
    start(yu, 1)
    start(yd, 1)
    start(yd, 2)
    start(xu, 1)
    start(xd, 1)
    start(yu, 2)
    start(zs, 2)
    start(yu, 3)
    start(yd, 3)
    start(xu, 2, 3, 4, 5)
    start(xd, 2, 3, 4, 5)

    def tokens(which):
        signal(token.at[which], [z_swap, z_far, core])
        pl.semaphore_wait(token.at[which], 3)

    begun = set()

    def product_of(slots, first, count, where):
        q = first * unit // depth
        span = slice(first * unit, (first + count) * unit)
        right = [f_all[at_slot(s), span, :] for s in slots]
        right = right[0] if len(right) == 1 else jnp.concatenate(right, axis=1)
        left = a_all[q, where, first * unit - q * depth : (first + count) * unit - q * depth]
        return jnp.dot(left, right, preferred_element_type=F32)

    def multiply(slots, first, count, chunks=(0, 1, 2)):
        base = CHUNKS[chunks[0]][0] * part_rows
        product = product_of(slots, first, count, slice(base, CHUNKS[chunks[-1]][1] * part_rows))
        width = product.shape[1] // len(slots)
        for i, slot in enumerate(slots):
            for c in chunks:
                s, begin, end = at_slot(slot), CHUNKS[c][0] * part_rows, CHUNKS[c][1] * part_rows
                term = product[begin - base : end - base, i * width : (i + 1) * width]
                acc[s, begin:end, :] = acc[s, begin:end, :] + term if (slot, c) in begun else term
                begun.add((slot, c))

    own_first = ((row * rows // depth - col + 4) % 4) * depth + (row * rows) % depth
    reds = []
    far_first = sorted(range(n_pole), key=lambda d: abs(d - n_pole // 2))

    def place(slot, total):
        wide[pl.ds(row_of(slot), rows, stride=8), :] = total

    def finish(pieces):
        totals = [acc[at_slot(slot)] + product_of([slot], first, count, slice(0, rows)) for slot, first, count in pieces]
        for (slot, _, _), total in zip(pieces, totals):
            near[NEAR.index(slot)] = weight_ref[0] * jnp.sum(row_sums(slot, total, 0), axis=0, keepdims=True)
            acc[at_slot(slot)] = total

    def tell_near(distances):
        for d in distances:
            for slot in NEAR:
                pltpu.make_async_remote_copy(
                    src_ref=near.at[NEAR.index(slot)],
                    dst_ref=late.at[NEAR.index(((-slot[0]) % 4, slot[1])), pole],
                    send_sem=end_send.at[0],
                    recv_sem=end_recv.at[0],
                    device_id={"pole": (pole + d) % n_pole, "row": row_of(slot)},
                    device_id_type=MESH,
                ).start()

    def tell_poles(distances):
        for d in distances:
            pltpu.make_async_remote_copy(
                src_ref=pol.at[pole],
                dst_ref=pol.at[pole],
                send_sem=end_send.at[1],
                recv_sem=end_recv.at[1],
                device_id={"pole": (pole + d) % n_pole},
                device_id_type=MESH,
            ).start()

    def row_sums(slot, total, first):
        count = total.shape[0]
        span = pl.ds(pl.multiple_of(own_first + first, 16), count)
        terms = f_all[at_slot(slot), span, :].astype(F32) * total
        return jnp.sum(terms.reshape(count // 8, 8, terms.shape[1]), axis=0)

    late_rows = CHUNKS[2][0] * part_rows

    def begin_rows(slot):
        part[at_slot(slot)] = row_sums(slot, acc[at_slot(slot), :late_rows, :], 0)

    def reduce_rows(slot):
        s = at_slot(slot)
        part[s] = part[s] + row_sums(slot, acc[s, late_rows:, :], late_rows)
        if slot == OWN:
            return
        back = at_slot(((-slot[0]) % 4, slot[1]))
        copy = pltpu.make_async_remote_copy(
            src_ref=part.at[s],
            dst_ref=red.at[back],
            send_sem=red_send.at[s],
            recv_sem=red_recv.at[back],
            device_id={"row": row_of(slot)},
            device_id_type=MESH,
        )
        copy.start()
        reds.append(copy)

    own_rows.wait()
    arrived(zs, 0)
    multiply([OWN, ZP], 0, 6)
    arrived(yu, 0, 1)
    start(yu, 4, 5)
    arrived(yd, 0, 1)
    start(zs, 3)
    start(yd, 4)
    tokens(0)
    arrived(yd, 2)
    start(yd, 5)
    arrived(xu, 0, 1, 2)
    start(xu, 6, 7, 8)
    arrived(xd, 0, 1, 2)
    start(xd, 6, 7, 8)
    arrived(zs, 1, 2)
    start(yu, 6, 7, 8)
    start(yd, 6, 7, 8)
    arrived(yu, 2)
    start(zs, 4)
    tokens(1)
    arrived(yu, 3)
    arrived(yd, 3)
    multiply([YN, YP], 0, 2)
    multiply([YP], 2, 4)
    tokens(2)
    arrived(yu, 4, 5)
    arrived(yd, 4, 5)
    start(zs, 5, 6, 7, 8, 9)
    tokens(3)
    arrived(xu, 3, 4, 5)
    arrived(xd, 3, 4, 5)
    multiply([OWN, ZP], 6, 6)
    multiply([OWN, ZP], 18, 2)
    multiply([OWN], 20, 4)
    arrived(yu, 6)
    start(yu, 9, 10, 11, 12)
    arrived(yd, 6)
    start(yd, 9, 10, 11, 12)
    multiply([YN, YP], 6, 2)
    multiply([YN], 8, 4)
    multiply([YN, YP], 18, 6)
    arrived(zs, 3, 4)
    multiply([YNZ, YPZ], 18, 6)
    arrived(yu, 7)
    arrived(yd, 7)
    multiply([YNZ, YPZ], 0, 6)
    multiply([YNZ, YPZ], 6, 6)
    arrived(xu, 6)
    arrived(xd, 6)
    arrived(yu, 8)
    arrived(yd, 8)
    arrived(zs, 5)
    multiply(SLOTS, 12, 6, (0,))
    arrived(yu, 9)
    arrived(yd, 9)
    arrived(zs, 6)
    multiply([YF, YFZ], 0, 3)
    multiply([YF, YFZ], 6, 3)
    multiply([YF, YFZ], 18, 3)
    arrived(xu, 7)
    arrived(xd, 7)
    multiply(SLOTS, 12, 6, (1,))
    arrived(yu, 10)
    arrived(yd, 10)
    arrived(zs, 7)
    multiply([YF, YFZ], 3, 3)
    multiply([YF, YFZ], 9, 3)
    multiply([YF, YFZ], 21, 3)
    for slot in FAR:
        begin_rows(slot)
    arrived(xu, 8)
    arrived(xd, 8)
    multiply(SLOTS, 12, 6, (2,))
    for slot in FAR:
        reduce_rows(slot)
    arrived(yu, 11)
    arrived(yd, 11)
    arrived(zs, 8)
    multiply([YP], 8, 3)
    multiply([YN], 2, 3)
    multiply([ZP], 20, 3)
    arrived(yu, 12)
    arrived(yd, 12)
    arrived(zs, 9)
    finish([(YP, 11, 1), (YN, 5, 1), (ZP, 23, 1)])

    tell_near(far_first[:3])
    for copy in reds:
        copy.wait_recv()
    total = part[at_slot(OWN)]
    for slot in (YNZ, YPZ, YF, YFZ):
        total = total + red[at_slot(slot)]
    pol[pole] = weight_ref[0] * (diag_ref[...] + jnp.sum(total, axis=0, keepdims=True))
    tell_poles(far_first[:3])
    tell_near(far_first[3:])
    tell_poles(far_first[3:-1])

    for slot in SLOTS:
        place(slot, acc[at_slot(slot)])

    def body(j, carry):
        base = pl.multiple_of(j * 32, 32)
        block = wide[pl.ds(pl.multiple_of(base * 8, 256), 256), :]
        out_ref[pl.ds(base, 32)] = (-block).reshape(32, 8, block.shape[1]).astype(BF16)
        return carry

    lax.fori_loop(0, rows // 32, body, 0)

    for copies in (yu, yd, zs, xu, xd, reds):
        for copy in copies:
            copy.wait_send()
    for i, whole in enumerate((late, pol.at[pl.ds(0, n_pole - 1)])):
        every = pltpu.make_async_remote_copy(
            src_ref=whole,
            dst_ref=whole,
            send_sem=end_send.at[i],
            recv_sem=end_recv.at[i],
            device_id=core,
            device_id_type=MESH,
        )
        every.wait()
    density = jnp.zeros(density_ref.shape, F32)
    for p in range(n_pole):
        density = density + ((pol[p] + late[0, p]) + (late[1, p] + late[2, p]))
    density_ref[...] = density


def hand_over(out_ref, density_ref, out_hbm, density_hbm, sems):
    rows = out_ref.shape[0]
    copies = [pltpu.make_async_copy(density_ref, density_hbm, sems.at[2])]
    for i in range(2):
        span = pl.ds(i * (rows // 2), rows // 2)
        copies.append(pltpu.make_async_copy(out_ref.at[span], out_hbm.at[span], sems.at[i]))
    for copy in copies:
        copy.start()
    for copy in copies:
        copy.wait()


def per_device(ancestor_inverse, factor_cols, diag_inverse, pole_weights, block_pattern, supernode_ids):
    _, rows, depth = ancestor_inverse.shape
    _, height, width = factor_cols.shape
    blocks = block_pattern.shape[0]
    vmem = pl.BlockSpec(memory_space=pltpu.VMEM)
    anywhere = pl.BlockSpec(memory_space=pl.ANY)
    dma = pltpu.SemaphoreType.DMA
    links = max(len(Y_UP), len(Z_SWAP))
    out, density = pl.pallas_call(
        kernel,
        out_shape=(
            pltpu.VMEM((rows, 8, width), BF16),
            pltpu.VMEM((1, width), F32),
        ),
        in_specs=[anywhere, anywhere, anywhere, pl.BlockSpec(memory_space=pltpu.SMEM), anywhere, anywhere],
        out_specs=(vmem, vmem),
        scratch_shapes=[
            pltpu.VMEM((4, rows, depth), BF16),
            pltpu.VMEM((8, height, width), BF16),
            pltpu.VMEM((8, rows, width), F32),
            pltpu.VMEM((blocks, width), F32),
            pltpu.VMEM((rows * 8 + 64, width), F32),
            pltpu.VMEM((1, width), F32),
            pltpu.VMEM(block_pattern.shape[::-1], jnp.int32),
            pltpu.VMEM((supernode_ids.size // width, width), jnp.int32),
            pltpu.VMEM((8, 8, width), F32),
            pltpu.VMEM((8, 8, width), F32),
            pltpu.VMEM((len(NEAR), 1, width), F32),
            pltpu.VMEM((len(NEAR), 8, 1, width), F32),
            pltpu.VMEM((8, 1, width), F32),
            dma((8,)),
            dma((3, links)),
            dma((3, links)),
            dma((2, len(X_UP))),
            dma((2, len(X_UP))),
            dma((8,)),
            dma((8,)),
            dma((2,)),
            dma((2,)),
            pltpu.SemaphoreType.REGULAR((ROUNDS,)),
        ],
        compiler_params=pltpu.CompilerParams(
            collective_id=0, has_side_effects=True, vmem_limit_bytes=63_400_000
        ),
        cost_estimate=pl.CostEstimate(
            flops=2 * rows * height * 8 * width, bytes_accessed=6 * 1024 * 1024, transcendentals=0
        ),
    )(
        ancestor_inverse,
        factor_cols,
        diag_inverse,
        pole_weights,
        block_pattern.T,
        supernode_ids.reshape(-1, width),
    )
    out, density = pl.pallas_call(
        hand_over,
        out_shape=(
            jax.ShapeDtypeStruct((rows, 8, width), BF16),
            jax.ShapeDtypeStruct((1, width), F32),
        ),
        in_specs=[vmem, vmem],
        out_specs=(anywhere, anywhere),
        scratch_shapes=[dma((3,))],
        compiler_params=pltpu.CompilerParams(vmem_limit_bytes=16 * 1024 * 1024),
    )(out, density)
    return out.reshape(1, rows, 8, 1, width), density.reshape(width)


def solution(mesh):
    in_specs = (
        P("pole", "row", "col"),
        P("pole", None, ("row", "col")),
        P("pole", ("row", "col")),
        P("pole"),
        P(),
        P(),
    )
    out_specs = (P("pole", "row", None, "col", None), P(("row", "col")))
    return jax.shard_map(per_device, mesh=mesh, in_specs=in_specs, out_specs=out_specs, check_vma=False)
```
